32 devices in a mesh: box: 8 (over z, x), grp: 4 (over y, core).
Axes of the slice: x: 2, y: 2, z: 4, core: 2. Of those that a mesh axis runs over, the one named last changes fastest.
Arguments:
- old_fields: float32 [3, 4, 32, 32, 1024], P(None, 'grp', 'box'), may hold values from -6 to 6, as said below
- old_count: int32 [4, 8], P('grp'), may hold values from 0 to 4, as said below
- neighbours: int32 [4, 16, 6], P('grp', 'box'), may hold values from -1 to 15, as said below
- parents: int32 [4, 16, 3], P('grp', 'box'), may hold values from 0 to 7, as said below
- coarse_source: float32 [4, 16, 8, 16, 256], P('grp', 'box'), may hold values from -6 to 6
Outputs:
- smoothed: float32 [4, 16, 32, 1024], P('grp', 'box')
- residual: float32 [4, 16, 32, 1024], P('grp', 'box')
- coarse_rhs: float32 [4, 16, 8, 16, 256], P('grp', 'box')
The draws below stay inside these ranges and needn't reach their ends.
Inputs may be any that keep to these rules, and one draw needn't show every extreme that they name: `old_fields`: components 0, 1, 2 are the solution, the right side and the cell coefficient; the coefficient lies in [0.25, 4]. `old_count`: in each owner group the counts sum to 16, and the sum of the first j counts differs from j * 2 by at most 1 for every j; some device holds 4 boxes and some none. Neighbourhood is symmetric; the x- neighbour of a box lies in the previous run of 2 boxes along the curve, the x+ neighbour in the next run, the y and z neighbours in the box's own run. `parents`: the named coarse box belongs to the owner on the same curve position as the fine box; no two fine boxes name the same octant of the same coarse box.
All inputs are finite; a program needn't handle non-finite values.
Results may differ from the reference program's by a relative error of at most 0.0001.
Values sent between devices are 32-bit elements; how exact they have to be, the bound alone decides.
A program may use at most 64 MiB of HBM per device.

```python
import math
import jax
import jax.numpy as jnp
from jax import lax

EDGE = 32
BOXES = 2
SLOTS = 4
COARSE_BOXES = 2
OWNERS = 4
CURVE = 8


def draw_old_fields(key, part):
    field_shape = (OWNERS, CURVE * SLOTS, EDGE, EDGE * EDGE)
    solution_key, source_key, weight_key = jax.random.split(key, 3)
    coefficient = jnp.exp(jax.random.uniform(weight_key, field_shape, jnp.float32, math.log(0.25), math.log(4.0)))
    solution = jnp.clip(jax.random.normal(solution_key, field_shape, jnp.float32), -6.0, 6.0)
    right_side = jnp.clip(jax.random.normal(source_key, field_shape, jnp.float32), -6.0, 6.0)
    return jnp.stack([solution, right_side, coefficient]).astype(jnp.float32)


def count_row(row_key):
    drift_key, low_key, high_key = jax.random.split(row_key, 3)
    spread = BOXES // 2
    drift = jax.random.randint(drift_key, (CURVE + 1,), -spread, spread + 1)
    low_place = jax.random.randint(low_key, (), 1, CURVE // 2)
    high_place = jax.random.randint(high_key, (), CURVE // 2 + 1, CURVE - 1)
    places = jnp.arange(CURVE + 1, dtype=jnp.int32)
    drift = jnp.where(places == low_place, -spread, drift)
    drift = jnp.where(places == low_place + 1, spread, drift)
    drift = jnp.where(places == high_place, spread, drift)
    drift = jnp.where(places == high_place + 1, -spread, drift)
    drift = jnp.where((places == 0) | (places == CURVE), 0, drift)
    return (BOXES + drift[1:] - drift[:-1]).astype(jnp.int32)


def draw_old_count(key, part):
    return jax.vmap(count_row)(jax.random.split(key, OWNERS)).astype(jnp.int32)


def neighbour_group(group_key):
    order_key, link_x_key, link_y_key, link_z_key = jax.random.split(group_key, 4)
    placing = jax.vmap(lambda one_key: jax.random.permutation(one_key, BOXES))(jax.random.split(order_key, CURVE)).astype(jnp.int32)
    slot_at = jnp.argsort(placing, axis=1, stable=True).astype(jnp.int32)
    curve_ids = jnp.arange(CURVE, dtype=jnp.int32)[:, None]
    place_ids = jnp.arange(BOXES, dtype=jnp.int32)[None, :]
    keep_x = (jax.random.randint(link_x_key, (CURVE, BOXES), 0, 4) > 0) & (curve_ids < CURVE - 1)
    keep_y = (jax.random.randint(link_y_key, (CURVE, BOXES), 0, 4) > 0) & (place_ids // 2 < BOXES // 2 - 1)
    keep_z = (jax.random.randint(link_z_key, (CURVE, BOXES), 0, 4) > 0) & (place_ids % 2 == 0)

    def lookup(row_step, place_step, linked):
        row_ids = jnp.clip(curve_ids + row_step, 0, CURVE - 1)
        place_new = jnp.clip(placing + place_step, 0, BOXES - 1)
        target = (curve_ids + row_step) * BOXES + slot_at[row_ids, place_new]
        return jnp.where(linked, target, -1)
    low_rows = jnp.clip(curve_ids - 1, 0, CURVE - 1)
    minus_x = lookup(-1, 0, (curve_ids > 0) & keep_x[low_rows, placing])
    plus_x = lookup(1, 0, keep_x[curve_ids, placing])
    minus_y = lookup(0, -2, (placing >= 2) & keep_y[curve_ids, jnp.clip(placing - 2, 0, BOXES - 1)])
    plus_y = lookup(0, 2, keep_y[curve_ids, placing])
    minus_z = lookup(0, -1, (placing % 2 == 1) & keep_z[curve_ids, jnp.clip(placing - 1, 0, BOXES - 1)])
    plus_z = lookup(0, 1, keep_z[curve_ids, placing])
    stacked = jnp.stack([minus_x, plus_x, minus_y, plus_y, minus_z, plus_z], axis=-1)
    return stacked.reshape(CURVE * BOXES, 6).astype(jnp.int32)


def draw_neighbours(key, part):
    return jax.vmap(neighbour_group)(jax.random.split(key, OWNERS)).astype(jnp.int32)


def parent_row(row_key):
    bias_key, score_key, order_key = jax.random.split(row_key, 3)
    triples = OWNERS * COARSE_BOXES * 8
    triple_ids = jnp.arange(triples, dtype=jnp.int32)
    bias = jax.random.randint(bias_key, (OWNERS,), 0, 4)
    owner_of = triple_ids // (COARSE_BOXES * 8)
    score = (jax.random.randint(score_key, (triples,), 0, 2 ** 14) + bias[owner_of] * 2 ** 13) * 1024 + triple_ids
    best_scores, best = lax.top_k(score, OWNERS * BOXES)
    chosen = best[jax.random.permutation(order_key, OWNERS * BOXES)]
    return jnp.stack([chosen // (COARSE_BOXES * 8), chosen // 8 % COARSE_BOXES, chosen % 8], axis=-1)


def draw_parents(key, part):
    rows_all = jax.vmap(parent_row)(jax.random.split(key, CURVE))
    rows_all = rows_all.reshape(CURVE, OWNERS, BOXES, 3).transpose(1, 0, 2, 3)
    return rows_all.reshape(OWNERS, CURVE * BOXES, 3).astype(jnp.int32)


def shard_levels(rng, dims, shards, least, top_value):
    loudness, own = 1.0, jax.random.fold_in(rng, 6)
    for position, shards_of in shards:
        steps = jnp.exp(jax.random.uniform(jax.random.fold_in(own, position), (shards_of,), jnp.float32, least / len(shards), top_value / len(shards)))
        loudness = loudness * jnp.repeat(steps, dims[position] // shards_of).reshape([-1 if axis == position else 1 for axis in range(len(dims))])
    return loudness


def gaussian(stream_key, extent, scale, limit, shards=(), kind=jnp.bfloat16):
    loudness = shard_levels(stream_key, extent, shards, -0.22, 0.18) if shards else 1.0
    values = jax.random.normal(stream_key, extent, jnp.float32) * scale * loudness
    return jnp.minimum(jnp.maximum(values, -limit), limit).astype(kind)


def setup_inputs(seed: int = 0) -> dict:
    seeds = jax.random.split(jax.random.key(seed), 6)
    return {
        "old_fields": draw_old_fields(jax.random.fold_in(seeds[5], 71), 0),
        "old_count": draw_old_count(jax.random.fold_in(seeds[5], 71), 0),
        "neighbours": draw_neighbours(jax.random.fold_in(seeds[5], 71), 0),
        "parents": draw_parents(jax.random.fold_in(seeds[5], 71), 0),
        "coarse_source": gaussian(seeds[4], (OWNERS, CURVE * COARSE_BOXES, 8, EDGE // 2, (EDGE // 2) * (EDGE // 2)), 1.0, 6.0, ((0, 4), (1, 8)), jnp.float32),
    }


MASS_TERM = 0.25


def cube_faces(box_cubes):
    return (box_cubes[:, 0], box_cubes[:, -1], box_cubes[:, :, 0], box_cubes[:, :, -1], box_cubes[:, :, :, 0], box_cubes[:, :, :, -1])


def ghost_faces(box_cubes, link_rows, keep_own):
    box_faces = cube_faces(box_cubes)
    results = []
    for face_id in range(6):
        across = box_faces[face_id ^ 1]
        target = link_rows[:, face_id]
        chosen = jnp.take(across, jnp.clip(target, 0, across.shape[0] - 1), axis=0)
        fallback = box_faces[face_id] if keep_own else jnp.zeros_like(chosen)
        results.append(jnp.where((target >= 0)[:, None, None], chosen, fallback))
    return results


def beside_cubes(box_cubes, ghosts):
    return (
        jnp.concatenate([ghosts[0][:, None], box_cubes[:, :-1]], axis=1),
        jnp.concatenate([box_cubes[:, 1:], ghosts[1][:, None]], axis=1),
        jnp.concatenate([ghosts[2][:, :, None], box_cubes[:, :, :-1]], axis=2),
        jnp.concatenate([box_cubes[:, :, 1:], ghosts[3][:, :, None]], axis=2),
        jnp.concatenate([ghosts[4][:, :, :, None], box_cubes[:, :, :, :-1]], axis=3),
        jnp.concatenate([box_cubes[:, :, :, 1:], ghosts[5][:, :, :, None]], axis=3),
    )


def weighted_sum(weights, nearby):
    running = weights[0] * nearby[0]
    for face_id in range(1, 6):
        running = running + weights[face_id] * nearby[face_id]
    return running


def reference(old_fields, old_count, neighbours, parents, coarse_source):
    box_edge = old_fields.shape[3]
    half_edge = box_edge // 2
    patch_boxes = CURVE * BOXES
    coarse_rhs = coarse_source
    smooth_list = []
    residual_list = []
    positions = jnp.arange(box_edge, dtype=jnp.int32)
    parity = (positions[:, None, None] + positions[None, :, None] + positions[None, None, :]) % 2
    for owner_index in range(OWNERS):
        counts = old_count[owner_index]
        run_ends = jnp.cumsum(counts)
        run_starts = run_ends - counts
        wanted = jnp.arange(patch_boxes, dtype=jnp.int32)
        source = jnp.sum((run_ends[None, :] <= wanted[:, None]).astype(jnp.int32), axis=1)
        old_rows = (source * SLOTS + wanted - jnp.take(run_starts, source)).astype(jnp.int32)
        moved_fields = jnp.take(old_fields[:, owner_index], old_rows, axis=1)
        moved_fields = moved_fields.reshape(3, patch_boxes, box_edge, box_edge, box_edge)
        solution = moved_fields[0]
        right_side = moved_fields[1]
        coefficient = moved_fields[2]
        link_rows = neighbours[owner_index]
        coef_near = beside_cubes(coefficient, ghost_faces(coefficient, link_rows, True))
        weights = [0.5 * (coefficient + nearby_coef) for nearby_coef in coef_near]
        diagonal = MASS_TERM + weights[0]
        for face_id in range(1, 6):
            diagonal = diagonal + weights[face_id]
        for sweep_step in range(4):
            nearby = beside_cubes(solution, ghost_faces(solution, link_rows, False))
            updated = (right_side + weighted_sum(weights, nearby)) / diagonal
            solution = jnp.where(parity == sweep_step % 2, updated, solution)
        nearby = beside_cubes(solution, ghost_faces(solution, link_rows, False))
        residual = right_side - (diagonal * solution - weighted_sum(weights, nearby))
        restricted = residual.reshape(patch_boxes, half_edge, 2, half_edge, 2, half_edge, 2).sum(axis=(2, 4, 6)) * 0.125
        restricted = restricted.reshape(patch_boxes, half_edge, half_edge * half_edge)
        owner_group = parents[owner_index, :, 0]
        coarse_box = (wanted // BOXES) * COARSE_BOXES + parents[owner_index, :, 1]
        coarse_rhs = coarse_rhs.at[owner_group, coarse_box, parents[owner_index, :, 2]].set(restricted)
        smooth_list.append(solution.reshape(patch_boxes, box_edge, box_edge * box_edge))
        residual_list.append(residual.reshape(patch_boxes, box_edge, box_edge * box_edge))
    return jnp.stack(smooth_list), jnp.stack(residual_list), coarse_rhs
```

```python
import jax
import jax.numpy as jnp
from jax import lax
from jax.experimental import pallas as pl
from jax.experimental.pallas import tpu as pltpu
from jax.sharding import PartitionSpec as P

MASS_TERM = 0.25
MESH = pl.DeviceIdType.MESH
LANES = 128
TILE = 8
PAD = 8
FACES = 6


def level_kernel(
    old_ref,
    count_ref,
    link_ref,
    parent_ref,
    coarse_ref,
    smooth_out,
    residual_out,
    coarse_out,
    held_sol,
    held_rhs,
    held_coef,
    send_right,
    sol,
    coef,
    weights,
    diagonal,
    scaled_rhs,
    plane_out,
    res_rows,
    merge_map,
    merged,
    pack,
    got_pack,
    coarse_buf,
    face_out,
    face_in,
    load_sem,
    move_send,
    move_recv,
    face_send,
    face_recv,
    pack_send,
    pack_recv,
    store_sem,
):
    place = lax.axis_index("box")
    group = lax.axis_index("grp")
    curve = lax.axis_size("box")
    groups = lax.axis_size("grp")
    slots = old_ref.shape[2]
    boxes = link_ref.shape[1]
    edge = old_ref.shape[3]
    cells = old_ref.shape[4]
    tiles = edge // TILE
    columns = cells // LANES
    half = edge // 2
    coarse_slots = coarse_buf.shape[0]
    has_left = place > 0
    has_right = place < curve - 1
    held = (held_sol, held_rhs, held_coef)

    def load(field):
        return pltpu.make_async_copy(
            old_ref.at[field, 0], held[field].at[pl.ds(0, slots)], load_sem.at[field]
        )

    coarse_load = pltpu.make_async_copy(coarse_ref, coarse_buf, load_sem.at[3])
    for field in (2, 0, 1):
        load(field).start()
    coarse_load.start()

    barrier = pltpu.get_barrier_semaphore()

    @pl.when(has_left)
    def _():
        pl.semaphore_signal(barrier, inc=1, device_id=(place - 1, group), device_id_type=MESH)

    @pl.when(has_right)
    def _():
        pl.semaphore_signal(barrier, inc=1, device_id=(place + 1, group), device_id_type=MESH)

    for step in range(1, groups):
        pl.semaphore_signal(
            barrier,
            inc=1,
            device_id=(place, lax.rem(group + step, groups)),
            device_id_type=MESH,
        )
    pl.semaphore_wait(
        barrier, groups - 1 + has_left.astype(jnp.int32) + has_right.astype(jnp.int32)
    )

    def move_left(field):
        return pltpu.make_async_remote_copy(
            src_ref=old_ref.at[field, 0, 0],
            dst_ref=held[field].at[slots + 1],
            send_sem=move_send.at[0, field],
            recv_sem=move_recv.at[0, field],
            device_id=(place - 1, group),
            device_id_type=MESH,
        )

    def move_right(field):
        return pltpu.make_async_remote_copy(
            src_ref=send_right.at[field],
            dst_ref=held[field].at[slots],
            send_sem=move_send.at[1, field],
            recv_sem=move_recv.at[1, field],
            device_id=(place + 1, group),
            device_id_type=MESH,
        )

    start = jnp.int32(0)
    for other in range(curve):
        start = start + jnp.where(other < place, count_ref[0, other], 0)
    end = start
    for other in range(curve):
        end = end + jnp.where(other == place, count_ref[0, other], 0)
    first = place * boxes
    right_slot = jnp.clip(first + boxes - start, 0, slots - 1)
    own_rows = []
    for b in range(boxes):
        wanted = first + b
        own = jnp.clip(wanted - start, 0, slots - 1)
        own_rows.append(
            jnp.where(wanted < start, slots, jnp.where(wanted >= end, slots + 1, own))
        )

    for field in (2, 0, 1):

        @pl.when(has_left)
        def _(field=field):
            move_left(field).start()

        load(field).wait()
        chosen = held[field][0]
        for s in range(1, slots):
            chosen = jnp.where(right_slot == s, held[field][s], chosen)
        send_right[field] = chosen

        @pl.when(has_right)
        def _(field=field):
            move_right(field).start()

    def move_wait(field):
        @pl.when(has_right)
        def _():
            move_left(field).wait_recv()

        @pl.when(has_left)
        def _():
            move_right(field).wait_recv()

    def face_to(k, side):
        return pltpu.make_async_remote_copy(
            src_ref=face_out.at[k, side],
            dst_ref=face_in.at[k, side],
            send_sem=face_send.at[k, side],
            recv_sem=face_recv.at[k, side],
            device_id=(place + 2 * side - 1, group),
            device_id_type=MESH,
        )

    def faces_start(k, ref):
        for b in range(boxes):
            face_out[k, 0, b] = ref[b, :, PAD : PAD + 1, :]
            face_out[k, 1, b] = ref[b, :, PAD + edge - 1 : PAD + edge, :]

        @pl.when(has_left)
        def _():
            face_to(k, 0).start()

        @pl.when(has_right)
        def _():
            face_to(k, 1).start()

    def faces_wait(k):
        @pl.when(has_left)
        def _():
            face_to(k, 1).wait_recv()

        @pl.when(has_right)
        def _():
            face_to(k, 0).wait_recv()

    links = [[link_ref[0, b, f] for f in range(FACES)] for b in range(boxes)]
    linked = [[jnp.where(t >= 0, 1.0, 0.0) for t in row] for row in links]
    beside = [[jnp.clip(t - first, 0, boxes - 1) for t in row] for row in links]

    def ghost_rows(k, ref, keep_own):
        for b in range(boxes):
            for f, side, base, row, own in (
                (0, 1, first - boxes, PAD - 1, PAD),
                (1, 0, first + boxes, PAD + edge, PAD + edge - 1),
            ):
                if keep_own:
                    plane = ref[b, :, own : own + 1, :]
                else:
                    plane = jnp.zeros((columns, 1, LANES), jnp.float32)
                for other in range(boxes):
                    plane = jnp.where(
                        (links[b][f] >= 0) & (links[b][f] == base + other),
                        face_in[k, side, other],
                        plane,
                    )
                ref[b, :, row : row + 1, :] = plane

    shape = (columns, TILE, LANES)
    lane = lax.broadcasted_iota(jnp.int32, shape, 2)
    column = lax.broadcasted_iota(jnp.int32, shape, 0)
    depth = lane & (edge - 1)
    low_depth = depth == 0
    high_depth = depth == edge - 1
    low_lane = lane < edge
    high_lane = lane >= LANES - edge
    low_row = low_lane & (column == 0)
    high_row = high_lane & (column == columns - 1)
    edge_masks = (None, None, low_row, high_row, low_depth, high_depth)
    parity = (
        lax.broadcasted_iota(jnp.int32, shape, 1)
        + column * (LANES // edge)
        + (lane >> (edge.bit_length() - 1))
        + depth
    ) & 1

    def around(ref, b, t):
        rows = slice(PAD + t * TILE, PAD + (t + 1) * TILE)
        here = ref[b, :, rows, :]
        low_y = pltpu.roll(here, edge, 2)
        high_y = pltpu.roll(here, LANES - edge, 2)
        ghost_low = pltpu.roll(ref[beside[b][2], columns - 1, rows, :], edge, 1)
        ghost_high = pltpu.roll(ref[beside[b][3], 0, rows, :], LANES - edge, 1)
        before = jnp.concatenate([ghost_low[None], low_y[:-1]], axis=0)
        after = jnp.concatenate([high_y[1:], ghost_high[None]], axis=0)
        return here, (
            ref[b, :, PAD + t * TILE - 1 : PAD + (t + 1) * TILE - 1, :],
            ref[b, :, PAD + t * TILE + 1 : PAD + (t + 1) * TILE + 1, :],
            jnp.where(low_lane, before, low_y),
            jnp.where(high_lane, after, high_y),
            jnp.where(
                low_depth,
                pltpu.roll(ref[beside[b][4], :, rows, :], LANES - edge + 1, 2),
                pltpu.roll(here, 1, 2),
            ),
            jnp.where(
                high_depth,
                pltpu.roll(ref[beside[b][5], :, rows, :], edge - 1, 2),
                pltpu.roll(here, LANES - 1, 2),
            ),
        )

    def spread(rows):
        return jnp.stack([rows[:, c * LANES : (c + 1) * LANES] for c in range(columns)])

    def flatten(block):
        return jnp.concatenate([block[c] for c in range(columns)], axis=1)

    target = lax.broadcasted_iota(jnp.int32, merge_map.shape, 0)
    target = ((target >> edge.bit_length()) * half) + (
        (target & (edge - 1)) >> 1
    )
    merge_map[...] = jnp.where(
        target == lax.broadcasted_iota(jnp.int32, merge_map.shape, 1), 1.0, 0.0
    ).astype(jnp.bfloat16)
    for b in range(boxes):
        label = (
            parent_ref[0, b, 0] * coarse_slots + parent_ref[0, b, 1] * 8 + parent_ref[0, b, 2]
        ).astype(jnp.float32)
        pack[b, half : half + TILE, :] = jnp.full((TILE, half * half), label, jnp.float32)

    def take(field, ref):
        for b in range(boxes):
            for t in range(tiles):
                ref[b, :, PAD + t * TILE : PAD + (t + 1) * TILE, :] = spread(
                    held[field][own_rows[b], t * TILE : (t + 1) * TILE, :]
                )

    move_wait(2)
    take(2, coef)
    faces_start(0, coef)
    move_wait(0)
    take(0, sol)
    faces_start(1, sol)
    faces_wait(0)
    ghost_rows(0, coef, True)
    for b in range(boxes):
        for t in range(tiles):
            here, near = around(coef, b, t)
            total = jnp.full(shape, MASS_TERM, jnp.float32)
            kept = []
            for f in range(FACES):
                beyond = near[f]
                if f >= 2:
                    inside = linked[b][f]
                    beyond = jnp.where(
                        edge_masks[f], beyond * inside + here * (1.0 - inside), beyond
                    )
                weight = 0.5 * (here + beyond)
                total = total + weight
                if f >= 2:
                    weight = jnp.where(edge_masks[f], weight * linked[b][f], weight)
                kept.append(weight)
            inverse = 1.0 / total
            diagonal[b, t] = total
            scaled_rhs[b, t] = inverse
            for f in range(FACES):
                weights[b, t, f] = kept[f] * inverse

    move_wait(1)
    for b in range(boxes):
        for t in range(tiles):
            scaled_rhs[b, t] = scaled_rhs[b, t] * spread(
                held[1][own_rows[b], t * TILE : (t + 1) * TILE, :]
            )

    def relaxed(b, t):
        here, near = around(sol, b, t)
        total = scaled_rhs[b, t]
        for f in range(FACES):
            total = total + weights[b, t, f] * near[f]
        return here, total

    inner = list(range(1, tiles - 1))
    outer = [0, tiles - 1] if tiles > 1 else [0]

    def sweep(colour, which):
        for b in range(boxes):
            for t in which:
                here, total = relaxed(b, t)
                sol[b, :, PAD + t * TILE : PAD + (t + 1) * TILE, :] = jnp.where(
                    parity == colour, total, here
                )

    for step in range(4):
        sweep(step % 2, inner)
        faces_wait(step + 1)
        ghost_rows(step + 1, sol, False)
        sweep(step % 2, outer)
        faces_start(step + 2, sol)

    for b in range(boxes):
        for t in range(tiles):
            plane_out[b, t * TILE : (t + 1) * TILE, :] = flatten(
                sol[b, :, PAD + t * TILE : PAD + (t + 1) * TILE, :]
            )
    smooth_store = pltpu.make_async_copy(plane_out, smooth_out.at[0], store_sem.at[0])
    smooth_store.start()

    def leave(which):
        for b in range(boxes):
            for t in which:
                here, total = relaxed(b, t)
                res_rows[b, t * TILE : (t + 1) * TILE, :] = flatten(
                    diagonal[b, t] * (total - here)
                )

    leave(inner)
    faces_wait(5)
    ghost_rows(5, sol, False)
    leave(outer)
    residual_store = pltpu.make_async_copy(res_rows, residual_out.at[0], store_sem.at[1])
    residual_store.start()

    for b in range(boxes):
        rows = res_rows[b]
        high = rows.astype(jnp.bfloat16)
        low = (rows - high.astype(jnp.float32)).astype(jnp.bfloat16)
        both = jnp.dot(
            jnp.concatenate([high, low], axis=0),
            merge_map[...],
            preferred_element_type=jnp.float32,
        )
        both = both[:edge] + both[edge:]
        for c in range(merged.shape[1]):
            merged[b, c] = both[:, c * LANES : (c + 1) * LANES]
    for b in range(boxes):
        for c in range(merged.shape[1]):
            pack[b, 0:half, c * LANES : (c + 1) * LANES] = 0.125 * (
                merged[b, c, pl.ds(0, half, stride=2), :]
                + merged[b, c, pl.ds(1, half, stride=2), :]
            )

    def pack_to(step):
        return pltpu.make_async_remote_copy(
            src_ref=pack,
            dst_ref=got_pack.at[step - 1],
            send_sem=pack_send.at[step - 1],
            recv_sem=pack_recv.at[step - 1],
            device_id=(place, lax.rem(group + step, groups)),
            device_id_type=MESH,
        )

    for step in range(1, groups):
        pack_to(step).start()
    coarse_load.wait()

    def place_from(refs):
        for ref in refs:
            for b in range(boxes):
                label = ref[b, half : half + TILE, :]
                label = jnp.concatenate([label] * (half // TILE), axis=0)
                values = ref[b, 0:half, :]

                def put(s, carry, label=label, values=values):
                    mine = (group * coarse_slots + s).astype(jnp.float32)
                    coarse_buf[s] = jnp.where(label == mine, values, coarse_buf[s])
                    return carry

                lax.fori_loop(0, coarse_slots, put, 0, unroll=True)

    place_from([pack])
    for step in range(1, groups):
        pack_to(step).wait_recv()
        place_from([got_pack.at[step - 1]])
    coarse_store = pltpu.make_async_copy(coarse_buf, coarse_out, store_sem.at[2])
    coarse_store.start()

    for step in range(1, groups):
        pack_to(step).wait_send()

    @pl.when(has_left)
    def _():
        for field in range(3):
            move_left(field).wait_send()
        for k in range(6):
            face_to(k, 0).wait_send()

    @pl.when(has_right)
    def _():
        for field in range(3):
            move_right(field).wait_send()
        for k in range(6):
            face_to(k, 1).wait_send()

    smooth_store.wait()
    residual_store.wait()
    coarse_store.wait()


def per_device(old_fields, old_count, neighbours, parents, coarse_source):
    fields, _, slots, edge, cells = old_fields.shape
    boxes = neighbours.shape[1]
    groups = lax.axis_size("grp")
    _, coarse_boxes, octants, half, quarter = coarse_source.shape
    tiles = edge // TILE
    columns = cells // LANES
    padded = edge + 2 * PAD
    f32 = jnp.float32
    coarse_slots = coarse_boxes * octants
    scratch = [
        pltpu.VMEM((slots + 2, edge, cells), f32),
        pltpu.VMEM((slots + 2, edge, cells), f32),
        pltpu.VMEM((slots + 2, edge, cells), f32),
        pltpu.VMEM((fields, edge, cells), f32),
        pltpu.VMEM((boxes, columns, padded, LANES), f32),
        pltpu.VMEM((boxes, columns, padded, LANES), f32),
        pltpu.VMEM((boxes, tiles, FACES, columns, TILE, LANES), f32),
        pltpu.VMEM((boxes, tiles, columns, TILE, LANES), f32),
        pltpu.VMEM((boxes, tiles, columns, TILE, LANES), f32),
        pltpu.VMEM((boxes, edge, cells), f32),
        pltpu.VMEM((boxes, edge, cells), f32),
        pltpu.VMEM((cells, quarter), jnp.bfloat16),
        pltpu.VMEM((boxes, quarter // LANES, edge, LANES), f32),
        pltpu.VMEM((boxes, half + TILE, quarter), f32),
        pltpu.VMEM((groups - 1, boxes, half + TILE, quarter), f32),
        pltpu.VMEM((coarse_slots, half, quarter), f32),
        pltpu.VMEM((6, 2, boxes, columns, 1, LANES), f32),
        pltpu.VMEM((6, 2, boxes, columns, 1, LANES), f32),
        pltpu.SemaphoreType.DMA((4,)),
        pltpu.SemaphoreType.DMA((2, 3)),
        pltpu.SemaphoreType.DMA((2, 3)),
        pltpu.SemaphoreType.DMA((6, 2)),
        pltpu.SemaphoreType.DMA((6, 2)),
        pltpu.SemaphoreType.DMA((groups - 1,)),
        pltpu.SemaphoreType.DMA((groups - 1,)),
        pltpu.SemaphoreType.DMA((3,)),
    ]
    anywhere = pl.BlockSpec(memory_space=pl.ANY)
    scalars = pl.BlockSpec(memory_space=pltpu.SMEM)
    smoothed, residual, coarse_rhs = pl.pallas_call(
        level_kernel,
        out_shape=(
            jax.ShapeDtypeStruct((1, boxes, edge, cells), f32),
            jax.ShapeDtypeStruct((1, boxes, edge, cells), f32),
            jax.ShapeDtypeStruct((coarse_slots, half, quarter), f32),
        ),
        in_specs=[anywhere, scalars, scalars, scalars, anywhere],
        out_specs=(anywhere, anywhere, anywhere),
        scratch_shapes=scratch,
        compiler_params=pltpu.CompilerParams(
            collective_id=0, has_side_effects=True, vmem_limit_bytes=48 * 1024 * 1024
        ),
    )(
        old_fields,
        old_count,
        neighbours,
        parents,
        coarse_source.reshape(coarse_slots, half, quarter),
    )
    return smoothed, residual, coarse_rhs.reshape(coarse_source.shape)


def solution(mesh):
    in_specs = (
        P(None, "grp", "box", None, None),
        P("grp", None),
        P("grp", "box", None),
        P("grp", "box", None),
        P("grp", "box", None, None, None),
    )
    out_specs = (
        P("grp", "box", None, None),
        P("grp", "box", None, None),
        P("grp", "box", None, None, None),
    )
    return jax.shard_map(
        per_device, mesh=mesh, in_specs=in_specs, out_specs=out_specs, check_vma=False
    )
```

```python
import jax
import jax.numpy as jnp
from jax import lax
from jax.experimental import pallas as pl
from jax.experimental.pallas import tpu as pltpu
from jax.sharding import PartitionSpec as P

MASS_TERM = 0.25
MESH = pl.DeviceIdType.MESH
LANES = 128
TILE = 8
PAD = 8
FACES = 6
VMEM_BYTES = 60 * 1024 * 1024


def level_kernel(
    old_ref,
    count_hbm,
    link_hbm,
    parent_hbm,
    coarse_ref,
    smooth_out,
    residual_out,
    coarse_out,
    count_ref,
    link_ref,
    parent_ref,
    held_sol,
    held_rhs,
    held_coef,
    coef_out,
    coef_in,
    half_out,
    half_in,
    sol,
    coef,
    weights,
    diagonal,
    inverse,
    scaled_rhs,
    plane_out,
    res_rows,
    merge_map,
    merged,
    pack,
    got_pack,
    coarse_buf,
    face_out,
    face_in,
    load_sem,
    move_send,
    move_recv,
    face_send,
    face_recv,
    pack_send,
    pack_recv,
    store_sem,
):
    place = lax.axis_index("box")
    group = lax.axis_index("grp")
    curve = lax.axis_size("box")
    groups = lax.axis_size("grp")
    slots = old_ref.shape[2]
    boxes = link_ref.shape[1]
    edge = old_ref.shape[3]
    cells = old_ref.shape[4]
    tiles = edge // TILE
    columns = cells // LANES
    half = edge // 2
    coarse_slots = coarse_buf.shape[0]
    has_left = place > 0
    has_right = place < curve - 1
    held = (held_sol, held_rhs, held_coef)

    def load(field):
        return pltpu.make_async_copy(old_ref.at[field, 0], held[field], load_sem.at[field])

    coarse_load = pltpu.make_async_copy(coarse_ref, coarse_buf, load_sem.at[3])
    tables = [
        pltpu.make_async_copy(source, target, load_sem.at[4 + i])
        for i, (source, target) in enumerate(
            ((count_hbm, count_ref), (link_hbm, link_ref), (parent_hbm, parent_ref))
        )
    ]
    barrier = pltpu.get_barrier_semaphore()

    @pl.when(has_left)
    def _():
        pl.semaphore_signal(barrier, inc=1, device_id=(place - 1, group), device_id_type=MESH)

    @pl.when(has_right)
    def _():
        pl.semaphore_signal(barrier, inc=1, device_id=(place + 1, group), device_id_type=MESH)

    for step in range(1, groups):
        pl.semaphore_signal(
            barrier,
            inc=1,
            device_id=(place, lax.rem(group + step, groups)),
            device_id_type=MESH,
        )
    for table in tables:
        table.start()
    for field in (2, 0, 1):
        load(field).start()
    coarse_load.start()

    shape = (columns, TILE, LANES)
    lane = lax.broadcasted_iota(jnp.int32, shape, 2)
    column = lax.broadcasted_iota(jnp.int32, shape, 0)
    depth = lane & (edge - 1)
    low_depth = depth == 0
    high_depth = depth == edge - 1
    low_lane = lane < edge
    high_lane = lane >= LANES - edge
    low_row = low_lane & (column == 0)
    high_row = high_lane & (column == columns - 1)
    edge_masks = (None, None, low_row, high_row, low_depth, high_depth)
    parity = (
        lax.broadcasted_iota(jnp.int32, shape, 1)
        + column * (LANES // edge)
        + (lane >> (edge.bit_length() - 1))
        + depth
    ) & 1
    pairs = columns // 2
    even_line = ((lane[:pairs] >> (edge.bit_length() - 1)) & 1) == 0
    odd_cell = parity[:pairs] == 1

    def spread(rows):
        return jnp.stack([rows[:, c * LANES : (c + 1) * LANES] for c in range(columns)])

    def flatten(block):
        return jnp.concatenate([block[c] for c in range(columns)], axis=1)

    def thin(block, colour):
        low, high = block[:pairs], block[pairs:]
        low_next = pltpu.roll(low, LANES - edge, 2)
        high_next = pltpu.roll(high, edge, 2)
        if colour:
            low = jnp.where(odd_cell, low, low_next)
            high = jnp.where(odd_cell, high, high_next)
        else:
            low = jnp.where(odd_cell, low_next, low)
            high = jnp.where(odd_cell, high_next, high)
        return jnp.where(even_line, low, high)

    def thicken(block):
        low = jnp.where(even_line, block, pltpu.roll(block, edge, 2))
        high = jnp.where(even_line, pltpu.roll(block, LANES - edge, 2), block)
        return jnp.concatenate([low, high], axis=0)

    for table in tables:
        table.wait()
    start = jnp.int32(0)
    for other in range(curve):
        start = start + jnp.where(other < place, count_ref[0, other], 0)
    end = start
    for other in range(curve):
        end = end + jnp.where(other == place, count_ref[0, other], 0)
    first = place * boxes
    right_slot = jnp.clip(first + boxes - start, 0, slots - 1)
    own_slots = [jnp.clip(first + b - start, 0, slots - 1) for b in range(boxes)]
    load(2).wait()
    for side, slot in ((0, 0), (1, right_slot)):
        coef_out[side] = held_coef[slot]
    pl.semaphore_wait(
        barrier, groups - 1 + has_left.astype(jnp.int32) + has_right.astype(jnp.int32)
    )

    def move(side, part):
        if part == 0:
            source, target = coef_out.at[side], coef_in.at[side]
        else:
            source, target = half_out.at[part - 1, side], half_in.at[part - 1, side]
        return pltpu.make_async_remote_copy(
            src_ref=source,
            dst_ref=target,
            send_sem=move_send.at[side, part],
            recv_sem=move_recv.at[side, part],
            device_id=(place + 2 * side - 1, group),
            device_id_type=MESH,
        )

    def move_start(part):
        @pl.when(has_left)
        def _():
            move(0, part).start()

        @pl.when(has_right)
        def _():
            move(1, part).start()

    def thin_out(part, field, colour):
        for side, slot in ((0, 0), (1, right_slot)):
            for t in range(tiles):
                rows = slice(t * TILE, (t + 1) * TILE)
                half_out[part - 1, side, :, rows, :] = thin(
                    spread(held[field][slot, rows, :]), colour
                )
        move_start(part)

    move_start(0)
    load(0).wait()
    thin_out(1, 0, 1)
    load(1).wait()
    thin_out(2, 1, 0)
    thin_out(3, 1, 1)

    def move_wait(part):
        @pl.when(has_right)
        def _():
            move(0, part).wait_recv()

        @pl.when(has_left)
        def _():
            move(1, part).wait_recv()

    def moved(field, b, t, arrived):
        rows = slice(t * TILE, (t + 1) * TILE)
        block = spread(held[field][own_slots[b], rows, :])
        if b == 0:
            block = jnp.where(first + b < start, arrived(1, rows), block)
        if b == boxes - 1:
            block = jnp.where(first + b >= end, arrived(0, rows), block)
        return block

    def face_to(k, side):
        return pltpu.make_async_remote_copy(
            src_ref=face_out.at[k, side],
            dst_ref=face_in.at[k, side],
            send_sem=face_send.at[k, side],
            recv_sem=face_recv.at[k, side],
            device_id=(place + 2 * side - 1, group),
            device_id_type=MESH,
        )

    def faces_start(k, ref):
        for b in range(boxes):
            face_out[k, 0, b] = ref[b, :, PAD : PAD + 1, :]
            face_out[k, 1, b] = ref[b, :, PAD + edge - 1 : PAD + edge, :]

        @pl.when(has_left)
        def _():
            face_to(k, 0).start()

        @pl.when(has_right)
        def _():
            face_to(k, 1).start()

    def faces_wait(k):
        @pl.when(has_left)
        def _():
            face_to(k, 1).wait_recv()

        @pl.when(has_right)
        def _():
            face_to(k, 0).wait_recv()

    links = [[link_ref[0, b, f] for f in range(FACES)] for b in range(boxes)]
    linked = [[jnp.where(t >= 0, 1.0, 0.0) for t in row] for row in links]
    beside = [[jnp.clip(t - first, 0, boxes - 1) for t in row] for row in links]

    def ghost_rows(k, ref, keep_own):
        for b in range(boxes):
            for f, side, base, row, own in (
                (0, 1, first - boxes, PAD - 1, PAD),
                (1, 0, first + boxes, PAD + edge, PAD + edge - 1),
            ):
                if keep_own:
                    plane = ref[b, :, own : own + 1, :]
                else:
                    plane = jnp.zeros((columns, 1, LANES), jnp.float32)
                for other in range(boxes):
                    plane = jnp.where(
                        (links[b][f] >= 0) & (links[b][f] == base + other),
                        face_in[k, side, other],
                        plane,
                    )
                ref[b, :, row : row + 1, :] = plane

    def around(ref, b, t):
        rows = slice(PAD + t * TILE, PAD + (t + 1) * TILE)
        here = ref[b, :, rows, :]
        low_y = pltpu.roll(here, edge, 2)
        high_y = pltpu.roll(here, LANES - edge, 2)
        ghost_low = pltpu.roll(ref[beside[b][2], columns - 1, rows, :], edge, 1)
        ghost_high = pltpu.roll(ref[beside[b][3], 0, rows, :], LANES - edge, 1)
        before = jnp.concatenate([ghost_low[None], low_y[:-1]], axis=0)
        after = jnp.concatenate([high_y[1:], ghost_high[None]], axis=0)
        return here, (
            ref[b, :, PAD + t * TILE - 1 : PAD + (t + 1) * TILE - 1, :],
            ref[b, :, PAD + t * TILE + 1 : PAD + (t + 1) * TILE + 1, :],
            jnp.where(low_lane, before, low_y),
            jnp.where(high_lane, after, high_y),
            jnp.where(
                low_depth,
                pltpu.roll(ref[beside[b][4], :, rows, :], LANES - edge + 1, 2),
                pltpu.roll(here, 1, 2),
            ),
            jnp.where(
                high_depth,
                pltpu.roll(ref[beside[b][5], :, rows, :], edge - 1, 2),
                pltpu.roll(here, LANES - 1, 2),
            ),
        )

    target = lax.broadcasted_iota(jnp.int32, merge_map.shape, 0)
    target = ((target >> edge.bit_length()) * half) + (
        (target & (edge - 1)) >> 1
    )
    merge_map[...] = jnp.where(
        target == lax.broadcasted_iota(jnp.int32, merge_map.shape, 1), 1.0, 0.0
    ).astype(jnp.bfloat16)
    for b in range(boxes):
        label = (
            parent_ref[0, b, 0] * coarse_slots + parent_ref[0, b, 1] * 8 + parent_ref[0, b, 2]
        ).astype(jnp.float32)
        pack[b, half : half + TILE, :] = jnp.full((TILE, half * half), label, jnp.float32)

    move_wait(0)
    for b in range(boxes):
        for t in range(tiles):
            coef[b, :, PAD + t * TILE : PAD + (t + 1) * TILE, :] = moved(
                2, b, t, lambda side, rows: spread(coef_in[side, rows, :])
            )
    faces_start(0, coef)
    move_wait(1)
    for b in range(boxes):
        for t in range(tiles):
            sol[b, :, PAD + t * TILE : PAD + (t + 1) * TILE, :] = moved(
                0, b, t, lambda side, rows: thicken(half_in[0, side, :, rows, :])
            )
    faces_start(1, sol)
    faces_wait(0)
    ghost_rows(0, coef, True)
    for b in range(boxes):
        for t in range(tiles):
            here, near = around(coef, b, t)
            total = jnp.full(shape, MASS_TERM, jnp.float32)
            kept = []
            for f in range(FACES):
                beyond = near[f]
                if f >= 2:
                    inside = linked[b][f]
                    beyond = jnp.where(
                        edge_masks[f], beyond * inside + here * (1.0 - inside), beyond
                    )
                weight = 0.5 * (here + beyond)
                total = total + weight
                if f >= 2:
                    weight = jnp.where(edge_masks[f], weight * linked[b][f], weight)
                kept.append(weight)
            over = 1.0 / total
            diagonal[b, t] = total
            inverse[b, t] = over
            for f in range(FACES):
                weights[b, t, f] = kept[f] * over

    def scale_rhs(part, arrived):
        move_wait(part)
        for b in range(boxes):
            for t in range(tiles):
                scaled_rhs[b, t] = inverse[b, t] * moved(1, b, t, arrived)

    def relaxed(b, t):
        here, near = around(sol, b, t)
        total = scaled_rhs[b, t]
        for f in range(FACES):
            total = total + weights[b, t, f] * near[f]
        return here, total

    inner = list(range(1, tiles - 1))
    outer = [0, tiles - 1] if tiles > 1 else [0]

    def sweep(colour, which):
        for b in range(boxes):
            for t in which:
                here, total = relaxed(b, t)
                sol[b, :, PAD + t * TILE : PAD + (t + 1) * TILE, :] = jnp.where(
                    parity == colour, total, here
                )

    scale_rhs(2, lambda side, rows: thicken(half_in[1, side, :, rows, :]))
    for step in range(4):
        if step == 1:
            scale_rhs(
                3,
                lambda side, rows: jnp.where(
                    parity == 0,
                    thicken(half_in[1, side, :, rows, :]),
                    thicken(half_in[2, side, :, rows, :]),
                ),
            )
        sweep(step % 2, inner)
        faces_wait(step + 1)
        ghost_rows(step + 1, sol, False)
        sweep(step % 2, outer)
        faces_start(step + 2, sol)

    for b in range(boxes):
        for t in range(tiles):
            plane_out[b, t * TILE : (t + 1) * TILE, :] = flatten(
                sol[b, :, PAD + t * TILE : PAD + (t + 1) * TILE, :]
            )
    smooth_store = pltpu.make_async_copy(plane_out, smooth_out.at[0], store_sem.at[0])
    smooth_store.start()

    def leave(which):
        for b in range(boxes):
            for t in which:
                here, total = relaxed(b, t)
                res_rows[b, t * TILE : (t + 1) * TILE, :] = flatten(
                    diagonal[b, t] * (total - here)
                )

    leave(inner)
    faces_wait(5)
    ghost_rows(5, sol, False)
    leave(outer)
    residual_store = pltpu.make_async_copy(res_rows, residual_out.at[0], store_sem.at[1])
    residual_store.start()

    for b in range(boxes):
        rows = res_rows[b]
        high = rows.astype(jnp.bfloat16)
        low = (rows - high.astype(jnp.float32)).astype(jnp.bfloat16)
        both = jnp.dot(
            jnp.concatenate([high, low], axis=0),
            merge_map[...],
            preferred_element_type=jnp.float32,
        )
        both = both[:edge] + both[edge:]
        for c in range(merged.shape[1]):
            merged[b, c] = both[:, c * LANES : (c + 1) * LANES]
    for b in range(boxes):
        for c in range(merged.shape[1]):
            pack[b, 0:half, c * LANES : (c + 1) * LANES] = 0.125 * (
                merged[b, c, pl.ds(0, half, stride=2), :]
                + merged[b, c, pl.ds(1, half, stride=2), :]
            )

    def pack_to(step):
        return pltpu.make_async_remote_copy(
            src_ref=pack,
            dst_ref=got_pack.at[step - 1],
            send_sem=pack_send.at[step - 1],
            recv_sem=pack_recv.at[step - 1],
            device_id=(place, lax.rem(group + step, groups)),
            device_id_type=MESH,
        )

    for step in range(1, groups):
        pack_to(step).start()
    coarse_load.wait()

    def place_from(refs):
        for ref in refs:
            for b in range(boxes):
                label = ref[b, half : half + TILE, :]
                label = jnp.concatenate([label] * (half // TILE), axis=0)
                values = ref[b, 0:half, :]

                def put(s, carry, label=label, values=values):
                    mine = (group * coarse_slots + s).astype(jnp.float32)
                    coarse_buf[s] = jnp.where(label == mine, values, coarse_buf[s])
                    return carry

                lax.fori_loop(0, coarse_slots, put, 0, unroll=True)

    place_from([pack])
    for step in range(1, groups):
        pack_to(step).wait_recv()
        place_from([got_pack.at[step - 1]])
    coarse_store = pltpu.make_async_copy(coarse_buf, coarse_out, store_sem.at[2])
    coarse_store.start()

    for step in range(1, groups):
        pack_to(step).wait_send()

    @pl.when(has_left)
    def _():
        for part in range(4):
            move(0, part).wait_send()
        for k in range(6):
            face_to(k, 0).wait_send()

    @pl.when(has_right)
    def _():
        for part in range(4):
            move(1, part).wait_send()
        for k in range(6):
            face_to(k, 1).wait_send()

    smooth_store.wait()
    residual_store.wait()
    coarse_store.wait()


def hand_out_kernel(*refs):
    sems = refs[6]
    copies = [pltpu.make_async_copy(refs[i], refs[3 + i], sems.at[i]) for i in range(3)]
    for copy in copies:
        copy.start()
    for copy in copies:
        copy.wait()


def per_device(old_fields, old_count, neighbours, parents, coarse_source):
    _, _, slots, edge, cells = old_fields.shape
    boxes = neighbours.shape[1]
    groups = lax.axis_size("grp")
    _, coarse_boxes, octants, half, quarter = coarse_source.shape
    tiles = edge // TILE
    columns = cells // LANES
    padded = edge + 2 * PAD
    f32 = jnp.float32
    coarse_slots = coarse_boxes * octants
    scratch = [
        pltpu.SMEM(old_count.shape, jnp.int32),
        pltpu.SMEM(neighbours.shape, jnp.int32),
        pltpu.SMEM(parents.shape, jnp.int32),
        pltpu.VMEM((slots, edge, cells), f32),
        pltpu.VMEM((slots, edge, cells), f32),
        pltpu.VMEM((slots, edge, cells), f32),
        pltpu.VMEM((2, edge, cells), f32),
        pltpu.VMEM((2, edge, cells), f32),
        pltpu.VMEM((3, 2, columns // 2, edge, LANES), f32),
        pltpu.VMEM((3, 2, columns // 2, edge, LANES), f32),
        pltpu.VMEM((boxes, columns, padded, LANES), f32),
        pltpu.VMEM((boxes, columns, padded, LANES), f32),
        pltpu.VMEM((boxes, tiles, FACES, columns, TILE, LANES), f32),
        pltpu.VMEM((boxes, tiles, columns, TILE, LANES), f32),
        pltpu.VMEM((boxes, tiles, columns, TILE, LANES), f32),
        pltpu.VMEM((boxes, tiles, columns, TILE, LANES), f32),
        pltpu.VMEM((boxes, edge, cells), f32),
        pltpu.VMEM((boxes, edge, cells), f32),
        pltpu.VMEM((cells, quarter), jnp.bfloat16),
        pltpu.VMEM((boxes, quarter // LANES, edge, LANES), f32),
        pltpu.VMEM((boxes, half + TILE, quarter), f32),
        pltpu.VMEM((groups - 1, boxes, half + TILE, quarter), f32),
        pltpu.VMEM((coarse_slots, half, quarter), f32),
        pltpu.VMEM((6, 2, boxes, columns, 1, LANES), f32),
        pltpu.VMEM((6, 2, boxes, columns, 1, LANES), f32),
        pltpu.SemaphoreType.DMA((7,)),
        pltpu.SemaphoreType.DMA((2, 4)),
        pltpu.SemaphoreType.DMA((2, 4)),
        pltpu.SemaphoreType.DMA((6, 2)),
        pltpu.SemaphoreType.DMA((6, 2)),
        pltpu.SemaphoreType.DMA((groups - 1,)),
        pltpu.SemaphoreType.DMA((groups - 1,)),
        pltpu.SemaphoreType.DMA((3,)),
    ]
    anywhere = pl.BlockSpec(memory_space=pl.ANY)
    in_hbm = pl.BlockSpec(memory_space=pltpu.HBM)
    smoothed, residual, coarse_rhs = pl.pallas_call(
        level_kernel,
        out_shape=(
            jax.ShapeDtypeStruct((1, boxes, edge, cells), f32),
            jax.ShapeDtypeStruct((1, boxes, edge, cells), f32),
            jax.ShapeDtypeStruct((coarse_slots, half, quarter), f32),
        ),
        in_specs=[in_hbm] * 5,
        out_specs=(anywhere, anywhere, anywhere),
        scratch_shapes=scratch,
        compiler_params=pltpu.CompilerParams(
            collective_id=0, has_side_effects=True, vmem_limit_bytes=VMEM_BYTES
        ),
    )(
        old_fields,
        old_count,
        neighbours,
        parents,
        coarse_source.reshape(coarse_slots, half, quarter),
    )
    results = (smoothed, residual, coarse_rhs)
    smoothed, residual, coarse_rhs = pl.pallas_call(
        hand_out_kernel,
        out_shape=tuple(jax.ShapeDtypeStruct(part.shape, f32) for part in results),
        in_specs=[anywhere] * 3,
        out_specs=(in_hbm,) * 3,
        scratch_shapes=[pltpu.SemaphoreType.DMA((3,))],
        compiler_params=pltpu.CompilerParams(vmem_limit_bytes=VMEM_BYTES),
    )(*results)
    return smoothed, residual, coarse_rhs.reshape(coarse_source.shape)


def solution(mesh):
    in_specs = (
        P(None, "grp", "box", None, None),
        P("grp", None),
        P("grp", "box", None),
        P("grp", "box", None),
        P("grp", "box", None, None, None),
    )
    out_specs = (
        P("grp", "box", None, None),
        P("grp", "box", None, None),
        P("grp", "box", None, None, None),
    )
    return jax.shard_map(
        per_device, mesh=mesh, in_specs=in_specs, out_specs=out_specs, check_vma=False
    )
```

```python
import functools

import jax
import jax.numpy as jnp
from jax import lax
from jax.experimental import pallas as pl
from jax.experimental.pallas import tpu as pltpu
from jax.sharding import PartitionSpec as P

MASS_TERM = 0.25
MESH = pl.DeviceIdType.MESH
LANES = 128
TILE = 8
PAD = 8
FACES = 6
VMEM_BYTES = 60 * 1024 * 1024


def level_kernel(
    coarse_slots,
    old_ref,
    count_hbm,
    link_hbm,
    parent_hbm,
    smooth_out,
    residual_out,
    packs_out,
    count_ref,
    link_ref,
    parent_ref,
    held_sol,
    held_rhs,
    held_coef,
    coef_out,
    coef_in,
    half_out,
    half_in,
    sol,
    coef,
    weights,
    diagonal,
    inverse,
    scaled_rhs,
    plane_out,
    res_rows,
    merge_map,
    merged,
    pack,
    face_out,
    face_in,
    load_sem,
    move_send,
    move_recv,
    face_send,
    face_recv,
    pack_send,
    pack_recv,
    store_sem,
):
    place = lax.axis_index("box")
    group = lax.axis_index("grp")
    curve = lax.axis_size("box")
    groups = lax.axis_size("grp")
    slots = old_ref.shape[2]
    boxes = link_ref.shape[1]
    edge = old_ref.shape[3]
    cells = old_ref.shape[4]
    tiles = edge // TILE
    columns = cells // LANES
    half = edge // 2
    has_left = place > 0
    has_right = place < curve - 1
    held = (held_sol, held_rhs, held_coef)

    def load(field):
        return pltpu.make_async_copy(old_ref.at[field, 0], held[field], load_sem.at[field])

    tables = [
        pltpu.make_async_copy(source, target, load_sem.at[3 + i])
        for i, (source, target) in enumerate(
            ((count_hbm, count_ref), (link_hbm, link_ref), (parent_hbm, parent_ref))
        )
    ]
    barrier = pltpu.get_barrier_semaphore()

    @pl.when(has_left)
    def _():
        pl.semaphore_signal(barrier, inc=1, device_id=(place - 1, group), device_id_type=MESH)

    @pl.when(has_right)
    def _():
        pl.semaphore_signal(barrier, inc=1, device_id=(place + 1, group), device_id_type=MESH)

    for step in range(1, groups):
        pl.semaphore_signal(
            barrier,
            inc=1,
            device_id=(place, lax.rem(group + step, groups)),
            device_id_type=MESH,
        )
    for table in tables:
        table.start()
    for field in (2, 0, 1):
        load(field).start()

    shape = (columns, TILE, LANES)
    lane = lax.broadcasted_iota(jnp.int32, shape, 2)
    column = lax.broadcasted_iota(jnp.int32, shape, 0)
    depth = lane & (edge - 1)
    low_depth = depth == 0
    high_depth = depth == edge - 1
    low_lane = lane < edge
    high_lane = lane >= LANES - edge
    low_row = low_lane & (column == 0)
    high_row = high_lane & (column == columns - 1)
    edge_masks = (None, None, low_row, high_row, low_depth, high_depth)
    parity = (
        lax.broadcasted_iota(jnp.int32, shape, 1)
        + column * (LANES // edge)
        + (lane >> (edge.bit_length() - 1))
        + depth
    ) & 1
    plane_shape = (columns, 1, LANES)
    plane_lane = lax.broadcasted_iota(jnp.int32, plane_shape, 2)
    plane_parity = (
        lax.broadcasted_iota(jnp.int32, plane_shape, 0) * (LANES // edge)
        + (plane_lane >> (edge.bit_length() - 1))
        + (plane_lane & (edge - 1))
    ) & 1
    pairs = columns // 2
    even_line = ((lane[:pairs] >> (edge.bit_length() - 1)) & 1) == 0
    odd_cell = parity[:pairs] == 1

    def spread(rows):
        return jnp.stack([rows[:, c * LANES : (c + 1) * LANES] for c in range(columns)])

    def flatten(block):
        return jnp.concatenate([block[c] for c in range(columns)], axis=1)

    def thin(block, colour):
        low, high = block[:pairs], block[pairs:]
        low_next = pltpu.roll(low, LANES - edge, 2)
        high_next = pltpu.roll(high, edge, 2)
        if colour:
            low = jnp.where(odd_cell, low, low_next)
            high = jnp.where(odd_cell, high, high_next)
        else:
            low = jnp.where(odd_cell, low_next, low)
            high = jnp.where(odd_cell, high_next, high)
        return jnp.where(even_line, low, high)

    def thicken(block):
        low = jnp.where(even_line, block, pltpu.roll(block, edge, 2))
        high = jnp.where(even_line, pltpu.roll(block, LANES - edge, 2), block)
        return jnp.concatenate([low, high], axis=0)

    for table in tables:
        table.wait()
    start = jnp.int32(0)
    for other in range(curve):
        start = start + jnp.where(other < place, count_ref[0, other], 0)
    end = start
    for other in range(curve):
        end = end + jnp.where(other == place, count_ref[0, other], 0)
    first = place * boxes
    right_slot = jnp.clip(first + boxes - start, 0, slots - 1)
    own_slots = [jnp.clip(first + b - start, 0, slots - 1) for b in range(boxes)]
    load(2).wait()
    for side, slot in ((0, 0), (1, right_slot)):
        coef_out[side] = held_coef[slot]
    pl.semaphore_wait(
        barrier, groups - 1 + has_left.astype(jnp.int32) + has_right.astype(jnp.int32)
    )

    def move(side, part):
        if part == 0:
            source, target = coef_out.at[side], coef_in.at[side]
        else:
            source, target = half_out.at[part - 1, side], half_in.at[part - 1, side]
        return pltpu.make_async_remote_copy(
            src_ref=source,
            dst_ref=target,
            send_sem=move_send.at[side, part],
            recv_sem=move_recv.at[side, part],
            device_id=(place + 2 * side - 1, group),
            device_id_type=MESH,
        )

    def move_start(part):
        @pl.when(has_left)
        def _():
            move(0, part).start()

        @pl.when(has_right)
        def _():
            move(1, part).start()

    def thin_out(part, field, colour):
        for side, slot in ((0, 0), (1, right_slot)):
            for t in range(tiles):
                rows = slice(t * TILE, (t + 1) * TILE)
                half_out[part - 1, side, :, rows, :] = thin(
                    spread(held[field][slot, rows, :]), colour
                )
        move_start(part)

    move_start(0)
    load(0).wait()
    thin_out(1, 0, 1)
    load(1).wait()
    thin_out(2, 1, 0)
    thin_out(3, 1, 1)

    def move_wait(part):
        @pl.when(has_right)
        def _():
            move(0, part).wait_recv()

        @pl.when(has_left)
        def _():
            move(1, part).wait_recv()

    def moved(field, b, t, arrived):
        rows = slice(t * TILE, (t + 1) * TILE)
        block = spread(held[field][own_slots[b], rows, :])
        if b == 0:
            block = jnp.where(first + b < start, arrived(1, rows), block)
        if b == boxes - 1:
            block = jnp.where(first + b >= end, arrived(0, rows), block)
        return block

    def face_to(k, side):
        return pltpu.make_async_remote_copy(
            src_ref=face_out.at[k, side],
            dst_ref=face_in.at[k, side],
            send_sem=face_send.at[k, side],
            recv_sem=face_recv.at[k, side],
            device_id=(place + 2 * side - 1, group),
            device_id_type=MESH,
        )

    def faces_start(k, plane_of):
        for b in range(boxes):
            for side in range(2):
                face_out[k, side, b] = plane_of(b, side)

        @pl.when(has_left)
        def _():
            face_to(k, 0).start()

        @pl.when(has_right)
        def _():
            face_to(k, 1).start()

    def faces_wait(k):
        @pl.when(has_left)
        def _():
            face_to(k, 1).wait_recv()

        @pl.when(has_right)
        def _():
            face_to(k, 0).wait_recv()

    def own_planes(ref):
        return lambda b, side: ref[
            b, :, PAD + side * (edge - 1) : PAD + side * (edge - 1) + 1, :
        ]

    links = [[link_ref[0, b, f] for f in range(FACES)] for b in range(boxes)]
    linked = [[jnp.where(t >= 0, 1.0, 0.0) for t in row] for row in links]
    beside = [[jnp.clip(t - first, 0, boxes - 1) for t in row] for row in links]

    def arrived_plane(k, b, f, plane):
        base = first + (2 * f - 1) * boxes
        for other in range(boxes):
            plane = jnp.where(
                (links[b][f] >= 0) & (links[b][f] == base + other),
                face_in[k, 1 - f, other],
                plane,
            )
        return plane

    no_plane = jnp.zeros((columns, 1, LANES), jnp.float32)
    ghost_at = (PAD - 1, PAD + edge)

    def ghost_rows(k, ref, keep_own):
        for b in range(boxes):
            for f in range(2):
                plane = own_planes(ref)(b, f) if keep_own else no_plane
                ref[b, :, ghost_at[f] : ghost_at[f] + 1, :] = arrived_plane(k, b, f, plane)

    def advance_ghosts(colour):
        for b in range(boxes):
            for f in range(2):
                row = slice(ghost_at[f], ghost_at[f] + 1)
                plane = sol[b, :, row, :]
                sol[b, :, row, :] = jnp.where(
                    ((plane_parity + 1 - f) & 1) == colour,
                    plane + arrived_plane(2, b, f, no_plane) * own_planes(sol)(b, f),
                    plane,
                )

    def around(ref, b, t):
        rows = slice(PAD + t * TILE, PAD + (t + 1) * TILE)
        here = ref[b, :, rows, :]
        low_y = pltpu.roll(here, edge, 2)
        high_y = pltpu.roll(here, LANES - edge, 2)
        ghost_low = pltpu.roll(ref[beside[b][2], columns - 1, rows, :], edge, 1)
        ghost_high = pltpu.roll(ref[beside[b][3], 0, rows, :], LANES - edge, 1)
        before = jnp.concatenate([ghost_low[None], low_y[:-1]], axis=0)
        after = jnp.concatenate([high_y[1:], ghost_high[None]], axis=0)
        return here, (
            ref[b, :, PAD + t * TILE - 1 : PAD + (t + 1) * TILE - 1, :],
            ref[b, :, PAD + t * TILE + 1 : PAD + (t + 1) * TILE + 1, :],
            jnp.where(low_lane, before, low_y),
            jnp.where(high_lane, after, high_y),
            jnp.where(
                low_depth,
                pltpu.roll(ref[beside[b][4], :, rows, :], LANES - edge + 1, 2),
                pltpu.roll(here, 1, 2),
            ),
            jnp.where(
                high_depth,
                pltpu.roll(ref[beside[b][5], :, rows, :], edge - 1, 2),
                pltpu.roll(here, LANES - 1, 2),
            ),
        )

    target = lax.broadcasted_iota(jnp.int32, merge_map.shape, 0)
    target = ((target >> edge.bit_length()) * half) + (
        (target & (edge - 1)) >> 1
    )
    merge_map[...] = jnp.where(
        target == lax.broadcasted_iota(jnp.int32, merge_map.shape, 1), 1.0, 0.0
    ).astype(jnp.bfloat16)
    for b in range(boxes):
        label = (
            parent_ref[0, b, 0] * coarse_slots + parent_ref[0, b, 1] * 8 + parent_ref[0, b, 2]
        ).astype(jnp.float32)
        pack[b, half : half + TILE, :] = jnp.full((TILE, half * half), label, jnp.float32)

    move_wait(0)
    for b in range(boxes):
        for t in range(tiles):
            coef[b, :, PAD + t * TILE : PAD + (t + 1) * TILE, :] = moved(
                2, b, t, lambda side, rows: spread(coef_in[side, rows, :])
            )
    faces_start(0, own_planes(coef))
    move_wait(1)
    for b in range(boxes):
        for t in range(tiles):
            sol[b, :, PAD + t * TILE : PAD + (t + 1) * TILE, :] = moved(
                0, b, t, lambda side, rows: thicken(half_in[0, side, :, rows, :])
            )
    faces_start(1, own_planes(sol))
    faces_wait(0)
    ghost_rows(0, coef, True)
    for b in range(boxes):
        for t in range(tiles):
            here, near = around(coef, b, t)
            total = jnp.full(shape, MASS_TERM, jnp.float32)
            kept = []
            for f in range(FACES):
                beyond = near[f]
                if f >= 2:
                    inside = linked[b][f]
                    beyond = jnp.where(
                        edge_masks[f], beyond * inside + here * (1.0 - inside), beyond
                    )
                weight = 0.5 * (here + beyond)
                total = total + weight
                if f >= 2:
                    weight = jnp.where(edge_masks[f], weight * linked[b][f], weight)
                kept.append(weight)
            over = 1.0 / total
            diagonal[b, t] = total
            inverse[b, t] = over
            for f in range(FACES):
                weights[b, t, f] = kept[f] * over

    faces_start(
        2,
        lambda b, side: weights[
            b, side * (tiles - 1), side, :, side * (TILE - 1) : side * (TILE - 1) + 1, :
        ],
    )

    def scale_rhs(part, arrived):
        move_wait(part)
        for b in range(boxes):
            for t in range(tiles):
                scaled_rhs[b, t] = inverse[b, t] * moved(1, b, t, arrived)

    def relaxed(b, t):
        here, near = around(sol, b, t)
        total = scaled_rhs[b, t]
        for f in range(FACES):
            total = total + weights[b, t, f] * near[f]
        return here, total

    inner = list(range(1, tiles - 1))
    outer = [0, tiles - 1] if tiles > 1 else [0]

    def sweep(colour, which):
        for b in range(boxes):
            for t in which:
                here, total = relaxed(b, t)
                sol[b, :, PAD + t * TILE : PAD + (t + 1) * TILE, :] = jnp.where(
                    parity == colour, total, here
                )

    scale_rhs(2, lambda side, rows: thicken(half_in[1, side, :, rows, :]))
    def next_planes(colour):
        def plane_of(b, side):
            t = side * (tiles - 1)
            here, near = around(sol, b, t)
            total = scaled_rhs[b, t]
            for f in range(FACES):
                if f != side:
                    total = total + weights[b, t, f] * near[f]
            block = jnp.where(parity == colour, total, here)
            return block[:, side * (TILE - 1) : side * (TILE - 1) + 1, :]

        return plane_of

    sweep(0, inner)
    faces_wait(1)
    ghost_rows(1, sol, False)
    sweep(0, outer)
    scale_rhs(
        3,
        lambda side, rows: jnp.where(
            parity == 0,
            thicken(half_in[1, side, :, rows, :]),
            thicken(half_in[2, side, :, rows, :]),
        ),
    )
    faces_start(3, next_planes(1))
    sweep(1, inner)
    faces_wait(2)
    faces_wait(3)
    ghost_rows(3, sol, False)
    sweep(1, outer)
    advance_ghosts(1)
    sweep(0, outer)
    faces_start(4, next_planes(1))
    sweep(0, inner)
    sweep(1, inner)
    faces_wait(4)
    ghost_rows(4, sol, False)
    sweep(1, outer)
    advance_ghosts(1)

    for b in range(boxes):
        for t in range(tiles):
            plane_out[b, t * TILE : (t + 1) * TILE, :] = flatten(
                sol[b, :, PAD + t * TILE : PAD + (t + 1) * TILE, :]
            )
    smooth_store = pltpu.make_async_copy(plane_out, smooth_out.at[0], store_sem.at[0])
    smooth_store.start()

    def leave(which):
        for b in range(boxes):
            for t in which:
                here, total = relaxed(b, t)
                res_rows[b, t * TILE : (t + 1) * TILE, :] = flatten(
                    diagonal[b, t] * (total - here)
                )

    leave(range(tiles))
    residual_store = pltpu.make_async_copy(res_rows, residual_out.at[0], store_sem.at[1])
    residual_store.start()

    for b in range(boxes):
        rows = res_rows[b]
        high = rows.astype(jnp.bfloat16)
        low = (rows - high.astype(jnp.float32)).astype(jnp.bfloat16)
        both = jnp.dot(
            jnp.concatenate([high, low], axis=0),
            merge_map[...],
            preferred_element_type=jnp.float32,
        )
        both = both[:edge] + both[edge:]
        for c in range(merged.shape[1]):
            merged[b, c] = both[:, c * LANES : (c + 1) * LANES]
    for b in range(boxes):
        for c in range(merged.shape[1]):
            pack[b, 0:half, c * LANES : (c + 1) * LANES] = 0.125 * (
                merged[b, c, pl.ds(0, half, stride=2), :]
                + merged[b, c, pl.ds(1, half, stride=2), :]
            )

    def pack_to(step):
        return pltpu.make_async_remote_copy(
            src_ref=pack,
            dst_ref=packs_out.at[step],
            send_sem=pack_send.at[step - 1],
            recv_sem=pack_recv.at[step - 1],
            device_id=(place, lax.rem(group + step, groups)),
            device_id_type=MESH,
        )

    for step in range(1, groups):
        pack_to(step).start()
    own_store = pltpu.make_async_copy(pack, packs_out.at[0], store_sem.at[2])
    own_store.start()
    for step in range(1, groups):
        pack_to(step).wait_recv()

    for step in range(1, groups):
        pack_to(step).wait_send()

    @pl.when(has_left)
    def _():
        for part in range(4):
            move(0, part).wait_send()
        for k in range(5):
            face_to(k, 0).wait_send()

    @pl.when(has_right)
    def _():
        for part in range(4):
            move(1, part).wait_send()
        for k in range(5):
            face_to(k, 1).wait_send()

    smooth_store.wait()
    residual_store.wait()
    own_store.wait()


def hand_out_kernel(
    smooth_in,
    residual_in,
    packs_in,
    coarse_in,
    smooth_out,
    residual_out,
    coarse_out,
    smooth_buf,
    residual_buf,
    packs,
    coarse,
    load_sem,
    store_sem,
):
    group = lax.axis_index("grp")
    groups, boxes = packs.shape[:2]
    slots, half = coarse.shape[:2]
    loads = [
        pltpu.make_async_copy(source, target, load_sem.at[i])
        for i, (source, target) in enumerate(
            (
                (packs_in, packs),
                (coarse_in, coarse),
                (smooth_in, smooth_buf),
                (residual_in, residual_buf),
            )
        )
    ]
    stores = [
        pltpu.make_async_copy(source, target, store_sem.at[i])
        for i, (source, target) in enumerate(
            ((smooth_buf, smooth_out), (residual_buf, residual_out), (coarse, coarse_out))
        )
    ]
    for load in loads:
        load.start()
    for load in loads:
        load.wait()
    stores[0].start()
    stores[1].start()
    for source in range(groups):
        for b in range(boxes):
            label = packs[source, b, half : half + TILE, :]
            label = jnp.concatenate([label] * (half // TILE), axis=0)
            values = packs[source, b, 0:half, :]
            for s in range(slots):
                mine = (group * slots + s).astype(jnp.float32)
                coarse[s] = jnp.where(label == mine, values, coarse[s])
    stores[2].start()
    for store in stores:
        store.wait()


def per_device(old_fields, old_count, neighbours, parents, coarse_source):
    _, _, slots, edge, cells = old_fields.shape
    boxes = neighbours.shape[1]
    groups = lax.axis_size("grp")
    _, coarse_boxes, octants, half, quarter = coarse_source.shape
    tiles = edge // TILE
    columns = cells // LANES
    padded = edge + 2 * PAD
    f32 = jnp.float32
    coarse_slots = coarse_boxes * octants
    scratch = [
        pltpu.SMEM(old_count.shape, jnp.int32),
        pltpu.SMEM(neighbours.shape, jnp.int32),
        pltpu.SMEM(parents.shape, jnp.int32),
        pltpu.VMEM((slots, edge, cells), f32),
        pltpu.VMEM((slots, edge, cells), f32),
        pltpu.VMEM((slots, edge, cells), f32),
        pltpu.VMEM((2, edge, cells), f32),
        pltpu.VMEM((2, edge, cells), f32),
        pltpu.VMEM((3, 2, columns // 2, edge, LANES), f32),
        pltpu.VMEM((3, 2, columns // 2, edge, LANES), f32),
        pltpu.VMEM((boxes, columns, padded, LANES), f32),
        pltpu.VMEM((boxes, columns, padded, LANES), f32),
        pltpu.VMEM((boxes, tiles, FACES, columns, TILE, LANES), f32),
        pltpu.VMEM((boxes, tiles, columns, TILE, LANES), f32),
        pltpu.VMEM((boxes, tiles, columns, TILE, LANES), f32),
        pltpu.VMEM((boxes, tiles, columns, TILE, LANES), f32),
        pltpu.VMEM((boxes, edge, cells), f32),
        pltpu.VMEM((boxes, edge, cells), f32),
        pltpu.VMEM((cells, quarter), jnp.bfloat16),
        pltpu.VMEM((boxes, quarter // LANES, edge, LANES), f32),
        pltpu.VMEM((boxes, half + TILE, quarter), f32),
        pltpu.VMEM((5, 2, boxes, columns, 1, LANES), f32),
        pltpu.VMEM((5, 2, boxes, columns, 1, LANES), f32),
        pltpu.SemaphoreType.DMA((6,)),
        pltpu.SemaphoreType.DMA((2, 4)),
        pltpu.SemaphoreType.DMA((2, 4)),
        pltpu.SemaphoreType.DMA((5, 2)),
        pltpu.SemaphoreType.DMA((5, 2)),
        pltpu.SemaphoreType.DMA((groups - 1,)),
        pltpu.SemaphoreType.DMA((groups - 1,)),
        pltpu.SemaphoreType.DMA((3,)),
    ]
    anywhere = pl.BlockSpec(memory_space=pl.ANY)
    in_hbm = pl.BlockSpec(memory_space=pltpu.HBM)
    smoothed, residual, packs = pl.pallas_call(
        functools.partial(level_kernel, coarse_slots),
        out_shape=(
            jax.ShapeDtypeStruct((1, boxes, edge, cells), f32),
            jax.ShapeDtypeStruct((1, boxes, edge, cells), f32),
            jax.ShapeDtypeStruct((groups, boxes, half + TILE, quarter), f32),
        ),
        in_specs=[in_hbm] * 4,
        out_specs=(anywhere, anywhere, anywhere),
        scratch_shapes=scratch,
        compiler_params=pltpu.CompilerParams(
            collective_id=0, has_side_effects=True, vmem_limit_bytes=VMEM_BYTES
        ),
    )(
        old_fields,
        old_count,
        neighbours,
        parents,
    )
    coarse = coarse_source.reshape(coarse_slots, half, quarter)
    parts = (smoothed, residual, packs, coarse)
    results = (smoothed, residual, coarse)
    smoothed, residual, coarse_rhs = pl.pallas_call(
        hand_out_kernel,
        out_shape=tuple(jax.ShapeDtypeStruct(part.shape, f32) for part in results),
        in_specs=[in_hbm] * 4,
        out_specs=(in_hbm,) * 3,
        scratch_shapes=[pltpu.VMEM(part.shape, f32) for part in parts]
        + [pltpu.SemaphoreType.DMA((4,)), pltpu.SemaphoreType.DMA((3,))],
        compiler_params=pltpu.CompilerParams(vmem_limit_bytes=VMEM_BYTES),
    )(*parts)
    return smoothed, residual, coarse_rhs.reshape(coarse_source.shape)


def solution(mesh):
    in_specs = (
        P(None, "grp", "box", None, None),
        P("grp", None),
        P("grp", "box", None),
        P("grp", "box", None),
        P("grp", "box", None, None, None),
    )
    out_specs = (
        P("grp", "box", None, None),
        P("grp", "box", None, None),
        P("grp", "box", None, None, None),
    )
    return jax.shard_map(
        per_device, mesh=mesh, in_specs=in_specs, out_specs=out_specs, check_vma=False
    )
```

```python
import functools

import jax
import jax.numpy as jnp
from jax import lax
from jax.experimental import pallas as pl
from jax.experimental.pallas import tpu as pltpu
from jax.sharding import PartitionSpec as P

MASS_TERM = 0.25
MESH = pl.DeviceIdType.MESH
LANES = 128
TILE = 8
PAD = 8
FACES = 6
VMEM_BYTES = 60 * 1024 * 1024


def level_kernel(
    coarse_slots,
    old_ref,
    count_hbm,
    link_hbm,
    parent_hbm,
    smooth_out,
    residual_out,
    packs_out,
    count_ref,
    link_ref,
    parent_ref,
    held_sol,
    held_rhs,
    held_coef,
    coef_out,
    coef_in,
    half_out,
    half_in,
    sol,
    coef,
    weights,
    diagonal,
    inverse,
    scaled_rhs,
    plane_out,
    res_rows,
    merge_map,
    merged,
    pack,
    face_out,
    face_in,
    load_sem,
    move_send,
    move_recv,
    face_send,
    face_recv,
    pack_send,
    pack_recv,
    store_sem,
):
    place = lax.axis_index("box")
    group = lax.axis_index("grp")
    curve = lax.axis_size("box")
    groups = lax.axis_size("grp")
    slots = old_ref.shape[2]
    boxes = link_ref.shape[1]
    edge = old_ref.shape[3]
    cells = old_ref.shape[4]
    tiles = edge // TILE
    columns = cells // LANES
    half = edge // 2
    has_left = place > 0
    has_right = place < curve - 1
    held = (held_sol, held_rhs, held_coef)

    def load(field):
        return pltpu.make_async_copy(old_ref.at[field, 0], held[field], load_sem.at[field])

    tables = [
        pltpu.make_async_copy(source, target, load_sem.at[3 + i])
        for i, (source, target) in enumerate(
            ((count_hbm, count_ref), (link_hbm, link_ref), (parent_hbm, parent_ref))
        )
    ]
    barrier = pltpu.get_barrier_semaphore()

    @pl.when(has_left)
    def _():
        pl.semaphore_signal(barrier, inc=1, device_id=(place - 1, group), device_id_type=MESH)

    @pl.when(has_right)
    def _():
        pl.semaphore_signal(barrier, inc=1, device_id=(place + 1, group), device_id_type=MESH)

    for step in range(1, groups):
        pl.semaphore_signal(
            barrier,
            inc=1,
            device_id=(place, lax.rem(group + step, groups)),
            device_id_type=MESH,
        )
    for table in tables:
        table.start()
    for field in (2, 0, 1):
        load(field).start()

    shape = (columns, TILE, LANES)
    lane = lax.broadcasted_iota(jnp.int32, shape, 2)
    column = lax.broadcasted_iota(jnp.int32, shape, 0)
    depth = lane & (edge - 1)
    low_depth = depth == 0
    high_depth = depth == edge - 1
    low_lane = lane < edge
    high_lane = lane >= LANES - edge
    low_row = low_lane & (column == 0)
    high_row = high_lane & (column == columns - 1)
    edge_masks = (None, None, low_row, high_row, low_depth, high_depth)
    parity = (
        lax.broadcasted_iota(jnp.int32, shape, 1)
        + column * (LANES // edge)
        + (lane >> (edge.bit_length() - 1))
        + depth
    ) & 1
    plane_shape = (columns, 1, LANES)
    plane_lane = lax.broadcasted_iota(jnp.int32, plane_shape, 2)
    plane_parity = (
        lax.broadcasted_iota(jnp.int32, plane_shape, 0) * (LANES // edge)
        + (plane_lane >> (edge.bit_length() - 1))
        + (plane_lane & (edge - 1))
    ) & 1
    pairs = columns // 2
    even_line = ((lane[:pairs] >> (edge.bit_length() - 1)) & 1) == 0
    odd_cell = parity[:pairs] == 1

    def spread(rows):
        return jnp.stack([rows[:, c * LANES : (c + 1) * LANES] for c in range(columns)])

    def flatten(block):
        return jnp.concatenate([block[c] for c in range(columns)], axis=1)

    def thin(block, colour):
        low, high = block[:pairs], block[pairs:]
        low_next = pltpu.roll(low, LANES - edge, 2)
        high_next = pltpu.roll(high, edge, 2)
        if colour:
            low = jnp.where(odd_cell, low, low_next)
            high = jnp.where(odd_cell, high, high_next)
        else:
            low = jnp.where(odd_cell, low_next, low)
            high = jnp.where(odd_cell, high_next, high)
        return jnp.where(even_line, low, high)

    def thicken(block):
        low = jnp.where(even_line, block, pltpu.roll(block, edge, 2))
        high = jnp.where(even_line, pltpu.roll(block, LANES - edge, 2), block)
        return jnp.concatenate([low, high], axis=0)

    for table in tables:
        table.wait()
    start = jnp.int32(0)
    for other in range(curve):
        start = start + jnp.where(other < place, count_ref[0, other], 0)
    end = start
    for other in range(curve):
        end = end + jnp.where(other == place, count_ref[0, other], 0)
    first = place * boxes
    right_slot = jnp.clip(first + boxes - start, 0, slots - 1)
    own_slots = [jnp.clip(first + b - start, 0, slots - 1) for b in range(boxes)]
    load(2).wait()
    for side, slot in ((0, 0), (1, right_slot)):
        coef_out[side] = held_coef[slot]
    pl.semaphore_wait(
        barrier, groups - 1 + has_left.astype(jnp.int32) + has_right.astype(jnp.int32)
    )

    def move(side, part):
        if part == 0:
            source, target = coef_out.at[side], coef_in.at[side]
        else:
            source, target = half_out.at[part - 1, side], half_in.at[part - 1, side]
        return pltpu.make_async_remote_copy(
            src_ref=source,
            dst_ref=target,
            send_sem=move_send.at[side, part],
            recv_sem=move_recv.at[side, part],
            device_id=(place + 2 * side - 1, group),
            device_id_type=MESH,
        )

    def move_start(part):
        @pl.when(has_left)
        def _():
            move(0, part).start()

        @pl.when(has_right)
        def _():
            move(1, part).start()

    def thin_out(part, field, colour):
        for side, slot in ((0, 0), (1, right_slot)):
            for t in range(tiles):
                rows = slice(t * TILE, (t + 1) * TILE)
                half_out[part - 1, side, :, rows, :] = thin(
                    spread(held[field][slot, rows, :]), colour
                )

    move_start(0)
    load(0).wait()
    thin_out(1, 0, 1)
    move_start(1)
    load(1).wait()
    thin_out(2, 1, 0)
    thin_out(3, 1, 1)

    def move_wait(part):
        @pl.when(has_right)
        def _():
            move(0, part).wait_recv()

        @pl.when(has_left)
        def _():
            move(1, part).wait_recv()

    def moved(field, b, t, arrived):
        rows = slice(t * TILE, (t + 1) * TILE)
        block = spread(held[field][own_slots[b], rows, :])
        if b == 0:
            block = jnp.where(first + b < start, arrived(1, rows), block)
        if b == boxes - 1:
            block = jnp.where(first + b >= end, arrived(0, rows), block)
        return block

    def face_to(k, side):
        return pltpu.make_async_remote_copy(
            src_ref=face_out.at[k, side],
            dst_ref=face_in.at[k, side],
            send_sem=face_send.at[k, side],
            recv_sem=face_recv.at[k, side],
            device_id=(place + 2 * side - 1, group),
            device_id_type=MESH,
        )

    def faces_start(k, plane_of):
        for b in range(boxes):
            for side in range(2):
                face_out[k, side, b] = plane_of(b, side)

        @pl.when(has_left)
        def _():
            face_to(k, 0).start()

        @pl.when(has_right)
        def _():
            face_to(k, 1).start()

    def faces_wait(k):
        @pl.when(has_left)
        def _():
            face_to(k, 1).wait_recv()

        @pl.when(has_right)
        def _():
            face_to(k, 0).wait_recv()

    def own_planes(ref):
        return lambda b, side: ref[
            b, :, PAD + side * (edge - 1) : PAD + side * (edge - 1) + 1, :
        ]

    links = [[link_ref[0, b, f] for f in range(FACES)] for b in range(boxes)]
    linked = [[jnp.where(t >= 0, 1.0, 0.0) for t in row] for row in links]
    beside = [[jnp.clip(t - first, 0, boxes - 1) for t in row] for row in links]

    def arrived_plane(k, b, f, plane):
        base = first + (2 * f - 1) * boxes
        for other in range(boxes):
            plane = jnp.where(
                (links[b][f] >= 0) & (links[b][f] == base + other),
                face_in[k, 1 - f, other],
                plane,
            )
        return plane

    no_plane = jnp.zeros((columns, 1, LANES), jnp.float32)
    ghost_at = (PAD - 1, PAD + edge)

    def ghost_rows(k, ref, keep_own):
        for b in range(boxes):
            for f in range(2):
                plane = own_planes(ref)(b, f) if keep_own else no_plane
                ref[b, :, ghost_at[f] : ghost_at[f] + 1, :] = arrived_plane(k, b, f, plane)

    def advance_ghosts(colour):
        for b in range(boxes):
            for f in range(2):
                row = slice(ghost_at[f], ghost_at[f] + 1)
                plane = sol[b, :, row, :]
                sol[b, :, row, :] = jnp.where(
                    ((plane_parity + 1 - f) & 1) == colour,
                    plane + arrived_plane(2, b, f, no_plane) * own_planes(sol)(b, f),
                    plane,
                )

    def around(ref, b, t):
        rows = slice(PAD + t * TILE, PAD + (t + 1) * TILE)
        here = ref[b, :, rows, :]
        low_y = pltpu.roll(here, edge, 2)
        high_y = pltpu.roll(here, LANES - edge, 2)
        ghost_low = pltpu.roll(ref[beside[b][2], columns - 1, rows, :], edge, 1)
        ghost_high = pltpu.roll(ref[beside[b][3], 0, rows, :], LANES - edge, 1)
        before = jnp.concatenate([ghost_low[None], low_y[:-1]], axis=0)
        after = jnp.concatenate([high_y[1:], ghost_high[None]], axis=0)
        return here, (
            ref[b, :, PAD + t * TILE - 1 : PAD + (t + 1) * TILE - 1, :],
            ref[b, :, PAD + t * TILE + 1 : PAD + (t + 1) * TILE + 1, :],
            jnp.where(low_lane, before, low_y),
            jnp.where(high_lane, after, high_y),
            jnp.where(
                low_depth,
                pltpu.roll(ref[beside[b][4], :, rows, :], LANES - edge + 1, 2),
                pltpu.roll(here, 1, 2),
            ),
            jnp.where(
                high_depth,
                pltpu.roll(ref[beside[b][5], :, rows, :], edge - 1, 2),
                pltpu.roll(here, LANES - 1, 2),
            ),
        )

    target = lax.broadcasted_iota(jnp.int32, merge_map.shape, 0)
    target = ((target >> edge.bit_length()) * half) + (
        (target & (edge - 1)) >> 1
    )
    merge_map[...] = jnp.where(
        target == lax.broadcasted_iota(jnp.int32, merge_map.shape, 1), 1.0, 0.0
    ).astype(jnp.bfloat16)
    for b in range(boxes):
        label = (
            parent_ref[0, b, 0] * coarse_slots + parent_ref[0, b, 1] * 8 + parent_ref[0, b, 2]
        ).astype(jnp.float32)
        pack[b, half : half + TILE, :] = jnp.full((TILE, half * half), label, jnp.float32)

    move_wait(0)
    for b in range(boxes):
        for t in range(tiles):
            coef[b, :, PAD + t * TILE : PAD + (t + 1) * TILE, :] = moved(
                2, b, t, lambda side, rows: spread(coef_in[side, rows, :])
            )
    faces_start(0, own_planes(coef))
    move_start(2)
    move_wait(1)
    for b in range(boxes):
        for t in range(tiles):
            sol[b, :, PAD + t * TILE : PAD + (t + 1) * TILE, :] = moved(
                0, b, t, lambda side, rows: thicken(half_in[0, side, :, rows, :])
            )
    faces_start(1, own_planes(sol))
    move_start(3)
    faces_wait(0)
    ghost_rows(0, coef, True)
    for b in range(boxes):
        for t in range(tiles):
            here, near = around(coef, b, t)
            total = jnp.full(shape, MASS_TERM, jnp.float32)
            kept = []
            for f in range(FACES):
                beyond = near[f]
                if f >= 2:
                    inside = linked[b][f]
                    beyond = jnp.where(
                        edge_masks[f], beyond * inside + here * (1.0 - inside), beyond
                    )
                weight = 0.5 * (here + beyond)
                total = total + weight
                if f >= 2:
                    weight = jnp.where(edge_masks[f], weight * linked[b][f], weight)
                kept.append(weight)
            over = 1.0 / total
            diagonal[b, t] = total
            inverse[b, t] = over
            for f in range(FACES):
                weights[b, t, f] = kept[f] * over

    faces_start(
        2,
        lambda b, side: weights[
            b, side * (tiles - 1), side, :, side * (TILE - 1) : side * (TILE - 1) + 1, :
        ],
    )

    def scale_rhs(part, arrived):
        move_wait(part)
        for b in range(boxes):
            for t in range(tiles):
                scaled_rhs[b, t] = inverse[b, t] * moved(1, b, t, arrived)

    def relaxed(b, t):
        here, near = around(sol, b, t)
        total = scaled_rhs[b, t]
        for f in range(FACES):
            total = total + weights[b, t, f] * near[f]
        return here, total

    inner = list(range(1, tiles - 1))
    outer = [0, tiles - 1] if tiles > 1 else [0]

    def sweep(colour, which):
        for b in range(boxes):
            for t in which:
                here, total = relaxed(b, t)
                sol[b, :, PAD + t * TILE : PAD + (t + 1) * TILE, :] = jnp.where(
                    parity == colour, total, here
                )

    scale_rhs(2, lambda side, rows: thicken(half_in[1, side, :, rows, :]))
    def next_planes(colour):
        def plane_of(b, side):
            t = side * (tiles - 1)
            here, near = around(sol, b, t)
            total = scaled_rhs[b, t]
            for f in range(FACES):
                if f != side:
                    total = total + weights[b, t, f] * near[f]
            block = jnp.where(parity == colour, total, here)
            return block[:, side * (TILE - 1) : side * (TILE - 1) + 1, :]

        return plane_of

    sweep(0, inner)
    faces_wait(1)
    ghost_rows(1, sol, False)
    sweep(0, outer)
    scale_rhs(
        3,
        lambda side, rows: jnp.where(
            parity == 0,
            thicken(half_in[1, side, :, rows, :]),
            thicken(half_in[2, side, :, rows, :]),
        ),
    )
    faces_start(3, next_planes(1))
    sweep(1, inner)
    faces_wait(2)
    faces_wait(3)
    ghost_rows(3, sol, False)
    sweep(1, outer)
    advance_ghosts(1)
    sweep(0, outer)
    faces_start(4, next_planes(1))
    sweep(0, inner)
    sweep(1, inner)
    faces_wait(4)
    ghost_rows(4, sol, False)
    sweep(1, outer)
    advance_ghosts(1)

    for b in range(boxes):
        for t in range(tiles):
            plane_out[b, t * TILE : (t + 1) * TILE, :] = flatten(
                sol[b, :, PAD + t * TILE : PAD + (t + 1) * TILE, :]
            )
    smooth_store = pltpu.make_async_copy(plane_out, smooth_out.at[0], store_sem.at[0])
    smooth_store.start()

    def leave(which):
        for b in range(boxes):
            for t in which:
                here, total = relaxed(b, t)
                res_rows[b, t * TILE : (t + 1) * TILE, :] = flatten(
                    diagonal[b, t] * (total - here)
                )

    leave(range(tiles))
    residual_store = pltpu.make_async_copy(res_rows, residual_out.at[0], store_sem.at[1])
    residual_store.start()

    for b in range(boxes):
        rows = res_rows[b]
        high = rows.astype(jnp.bfloat16)
        low = (rows - high.astype(jnp.float32)).astype(jnp.bfloat16)
        both = jnp.dot(
            jnp.concatenate([high, low], axis=0),
            merge_map[...],
            preferred_element_type=jnp.float32,
        )
        both = both[:edge] + both[edge:]
        for c in range(merged.shape[1]):
            merged[b, c] = both[:, c * LANES : (c + 1) * LANES]
    for b in range(boxes):
        for c in range(merged.shape[1]):
            pack[b, 0:half, c * LANES : (c + 1) * LANES] = 0.125 * (
                merged[b, c, pl.ds(0, half, stride=2), :]
                + merged[b, c, pl.ds(1, half, stride=2), :]
            )

    def pack_to(step):
        return pltpu.make_async_remote_copy(
            src_ref=pack,
            dst_ref=packs_out.at[step],
            send_sem=pack_send.at[step - 1],
            recv_sem=pack_recv.at[step - 1],
            device_id=(place, lax.rem(group + step, groups)),
            device_id_type=MESH,
        )

    for step in range(1, groups):
        pack_to(step).start()
    own_store = pltpu.make_async_copy(pack, packs_out.at[0], store_sem.at[2])
    own_store.start()
    for step in range(1, groups):
        pack_to(step).wait_recv()

    for step in range(1, groups):
        pack_to(step).wait_send()

    @pl.when(has_left)
    def _():
        for part in range(4):
            move(0, part).wait_send()
        for k in range(5):
            face_to(k, 0).wait_send()

    @pl.when(has_right)
    def _():
        for part in range(4):
            move(1, part).wait_send()
        for k in range(5):
            face_to(k, 1).wait_send()

    smooth_store.wait()
    residual_store.wait()
    own_store.wait()


def hand_out_kernel(
    smooth_in,
    residual_in,
    packs_in,
    coarse_in,
    smooth_out,
    residual_out,
    coarse_out,
    smooth_buf,
    residual_buf,
    packs,
    coarse,
    load_sem,
    store_sem,
):
    group = lax.axis_index("grp")
    groups, boxes = packs.shape[:2]
    slots, half = coarse.shape[:2]
    loads = [
        pltpu.make_async_copy(source, target, load_sem.at[i])
        for i, (source, target) in enumerate(
            (
                (packs_in, packs),
                (coarse_in, coarse),
                (smooth_in, smooth_buf),
                (residual_in, residual_buf),
            )
        )
    ]
    stores = [
        pltpu.make_async_copy(source, target, store_sem.at[i])
        for i, (source, target) in enumerate(
            ((smooth_buf, smooth_out), (residual_buf, residual_out), (coarse, coarse_out))
        )
    ]
    for load in loads:
        load.start()
    for load in loads:
        load.wait()
    stores[0].start()
    stores[1].start()
    for source in range(groups):
        for b in range(boxes):
            label = packs[source, b, half : half + TILE, :]
            label = jnp.concatenate([label] * (half // TILE), axis=0)
            values = packs[source, b, 0:half, :]
            for s in range(slots):
                mine = (group * slots + s).astype(jnp.float32)
                coarse[s] = jnp.where(label == mine, values, coarse[s])
    stores[2].start()
    for store in stores:
        store.wait()


def per_device(old_fields, old_count, neighbours, parents, coarse_source):
    _, _, slots, edge, cells = old_fields.shape
    boxes = neighbours.shape[1]
    groups = lax.axis_size("grp")
    _, coarse_boxes, octants, half, quarter = coarse_source.shape
    tiles = edge // TILE
    columns = cells // LANES
    padded = edge + 2 * PAD
    f32 = jnp.float32
    coarse_slots = coarse_boxes * octants
    scratch = [
        pltpu.SMEM(old_count.shape, jnp.int32),
        pltpu.SMEM(neighbours.shape, jnp.int32),
        pltpu.SMEM(parents.shape, jnp.int32),
        pltpu.VMEM((slots, edge, cells), f32),
        pltpu.VMEM((slots, edge, cells), f32),
        pltpu.VMEM((slots, edge, cells), f32),
        pltpu.VMEM((2, edge, cells), f32),
        pltpu.VMEM((2, edge, cells), f32),
        pltpu.VMEM((3, 2, columns // 2, edge, LANES), f32),
        pltpu.VMEM((3, 2, columns // 2, edge, LANES), f32),
        pltpu.VMEM((boxes, columns, padded, LANES), f32),
        pltpu.VMEM((boxes, columns, padded, LANES), f32),
        pltpu.VMEM((boxes, tiles, FACES, columns, TILE, LANES), f32),
        pltpu.VMEM((boxes, tiles, columns, TILE, LANES), f32),
        pltpu.VMEM((boxes, tiles, columns, TILE, LANES), f32),
        pltpu.VMEM((boxes, tiles, columns, TILE, LANES), f32),
        pltpu.VMEM((boxes, edge, cells), f32),
        pltpu.VMEM((boxes, edge, cells), f32),
        pltpu.VMEM((cells, quarter), jnp.bfloat16),
        pltpu.VMEM((boxes, quarter // LANES, edge, LANES), f32),
        pltpu.VMEM((boxes, half + TILE, quarter), f32),
        pltpu.VMEM((5, 2, boxes, columns, 1, LANES), f32),
        pltpu.VMEM((5, 2, boxes, columns, 1, LANES), f32),
        pltpu.SemaphoreType.DMA((6,)),
        pltpu.SemaphoreType.DMA((2, 4)),
        pltpu.SemaphoreType.DMA((2, 4)),
        pltpu.SemaphoreType.DMA((5, 2)),
        pltpu.SemaphoreType.DMA((5, 2)),
        pltpu.SemaphoreType.DMA((groups - 1,)),
        pltpu.SemaphoreType.DMA((groups - 1,)),
        pltpu.SemaphoreType.DMA((3,)),
    ]
    anywhere = pl.BlockSpec(memory_space=pl.ANY)
    in_hbm = pl.BlockSpec(memory_space=pltpu.HBM)
    smoothed, residual, packs = pl.pallas_call(
        functools.partial(level_kernel, coarse_slots),
        out_shape=(
            jax.ShapeDtypeStruct((1, boxes, edge, cells), f32),
            jax.ShapeDtypeStruct((1, boxes, edge, cells), f32),
            jax.ShapeDtypeStruct((groups, boxes, half + TILE, quarter), f32),
        ),
        in_specs=[in_hbm] * 4,
        out_specs=(anywhere, anywhere, anywhere),
        scratch_shapes=scratch,
        compiler_params=pltpu.CompilerParams(
            collective_id=0, has_side_effects=True, vmem_limit_bytes=VMEM_BYTES
        ),
    )(
        old_fields,
        old_count,
        neighbours,
        parents,
    )
    coarse = coarse_source.reshape(coarse_slots, half, quarter)
    parts = (smoothed, residual, packs, coarse)
    results = (smoothed, residual, coarse)
    smoothed, residual, coarse_rhs = pl.pallas_call(
        hand_out_kernel,
        out_shape=tuple(jax.ShapeDtypeStruct(part.shape, f32) for part in results),
        in_specs=[in_hbm] * 4,
        out_specs=(in_hbm,) * 3,
        scratch_shapes=[pltpu.VMEM(part.shape, f32) for part in parts]
        + [pltpu.SemaphoreType.DMA((4,)), pltpu.SemaphoreType.DMA((3,))],
        compiler_params=pltpu.CompilerParams(vmem_limit_bytes=VMEM_BYTES),
    )(*parts)
    return smoothed, residual, coarse_rhs.reshape(coarse_source.shape)


def solution(mesh):
    in_specs = (
        P(None, "grp", "box", None, None),
        P("grp", None),
        P("grp", "box", None),
        P("grp", "box", None),
        P("grp", "box", None, None, None),
    )
    out_specs = (
        P("grp", "box", None, None),
        P("grp", "box", None, None),
        P("grp", "box", None, None, None),
    )
    return jax.shard_map(
        per_device, mesh=mesh, in_specs=in_specs, out_specs=out_specs, check_vma=False
    )
```

```python
import functools

import jax
import jax.numpy as jnp
from jax import lax
from jax.experimental import pallas as pl
from jax.experimental.pallas import tpu as pltpu
from jax.sharding import PartitionSpec as P

MASS_TERM = 0.25
MESH = pl.DeviceIdType.MESH
LANES = 128
TILE = 8
PAD = 8
FACES = 6
VMEM_BYTES = 60 * 1024 * 1024


def level_kernel(
    coarse_slots,
    old_ref,
    count_hbm,
    link_hbm,
    parent_hbm,
    smooth_out,
    residual_out,
    packs_out,
    count_ref,
    link_ref,
    parent_ref,
    held_sol,
    held_rhs,
    held_coef,
    coef_out,
    coef_in,
    half_out,
    half_in,
    rows_out,
    rows_in,
    sol,
    coef,
    weights,
    diagonal,
    inverse,
    scaled_rhs,
    plane_out,
    res_rows,
    merge_map,
    merged,
    pack,
    face_out,
    face_in,
    load_sem,
    move_send,
    move_recv,
    face_send,
    face_recv,
    pack_send,
    pack_recv,
    store_sem,
):
    place = lax.axis_index("box")
    group = lax.axis_index("grp")
    curve = lax.axis_size("box")
    groups = lax.axis_size("grp")
    slots = old_ref.shape[2]
    boxes = link_ref.shape[1]
    edge = old_ref.shape[3]
    cells = old_ref.shape[4]
    tiles = edge // TILE
    columns = cells // LANES
    half = edge // 2
    has_left = place > 0
    has_right = place < curve - 1
    held = (held_sol, held_rhs, held_coef)

    def load(field):
        return pltpu.make_async_copy(old_ref.at[field, 0], held[field], load_sem.at[field])

    tables = [
        pltpu.make_async_copy(source, target, load_sem.at[3 + i])
        for i, (source, target) in enumerate(
            ((count_hbm, count_ref), (link_hbm, link_ref), (parent_hbm, parent_ref))
        )
    ]
    barrier = pltpu.get_barrier_semaphore()

    @pl.when(has_left)
    def _():
        pl.semaphore_signal(barrier, inc=1, device_id=(place - 1, group), device_id_type=MESH)

    @pl.when(has_right)
    def _():
        pl.semaphore_signal(barrier, inc=1, device_id=(place + 1, group), device_id_type=MESH)

    for step in range(1, groups):
        pl.semaphore_signal(
            barrier,
            inc=1,
            device_id=(place, lax.rem(group + step, groups)),
            device_id_type=MESH,
        )
    for table in tables:
        table.start()
    for field in (2, 0, 1):
        load(field).start()

    shape = (columns, TILE, LANES)
    lane = lax.broadcasted_iota(jnp.int32, shape, 2)
    column = lax.broadcasted_iota(jnp.int32, shape, 0)
    depth = lane & (edge - 1)
    low_depth = depth == 0
    high_depth = depth == edge - 1
    low_lane = lane < edge
    high_lane = lane >= LANES - edge
    low_row = low_lane & (column == 0)
    high_row = high_lane & (column == columns - 1)
    edge_masks = (None, None, low_row, high_row, low_depth, high_depth)
    parity = (
        lax.broadcasted_iota(jnp.int32, shape, 1)
        + column * (LANES // edge)
        + (lane >> (edge.bit_length() - 1))
        + depth
    ) & 1
    plane_shape = (columns, 1, LANES)
    plane_lane = lax.broadcasted_iota(jnp.int32, plane_shape, 2)
    plane_parity = (
        lax.broadcasted_iota(jnp.int32, plane_shape, 0) * (LANES // edge)
        + (plane_lane >> (edge.bit_length() - 1))
        + (plane_lane & (edge - 1))
    ) & 1
    pairs = columns // 2
    even_line = ((lane[:pairs] >> (edge.bit_length() - 1)) & 1) == 0
    odd_cell = parity[:pairs] == 1

    def spread(rows):
        return jnp.stack([rows[:, c * LANES : (c + 1) * LANES] for c in range(columns)])

    def flatten(block):
        return jnp.concatenate([block[c] for c in range(columns)], axis=1)

    def thin(block, colour):
        low, high = block[:pairs], block[pairs:]
        low_next = pltpu.roll(low, LANES - edge, 2)
        high_next = pltpu.roll(high, edge, 2)
        if colour:
            low = jnp.where(odd_cell, low, low_next)
            high = jnp.where(odd_cell, high, high_next)
        else:
            low = jnp.where(odd_cell, low_next, low)
            high = jnp.where(odd_cell, high_next, high)
        return jnp.where(even_line, low, high)

    def thicken(block):
        low = jnp.where(even_line, block, pltpu.roll(block, edge, 2))
        high = jnp.where(even_line, pltpu.roll(block, LANES - edge, 2), block)
        return jnp.concatenate([low, high], axis=0)

    for table in tables:
        table.wait()
    start = jnp.int32(0)
    for other in range(curve):
        start = start + jnp.where(other < place, count_ref[0, other], 0)
    end = start
    for other in range(curve):
        end = end + jnp.where(other == place, count_ref[0, other], 0)
    first = place * boxes
    right_slot = jnp.clip(first + boxes - start, 0, slots - 1)
    own_slots = [jnp.clip(first + b - start, 0, slots - 1) for b in range(boxes)]
    load(2).wait()
    for side, slot in ((0, 0), (1, right_slot)):
        coef_out[side] = held_coef[slot]
    pl.semaphore_wait(
        barrier, groups - 1 + has_left.astype(jnp.int32) + has_right.astype(jnp.int32)
    )

    def move(side, part):
        if part == 0:
            source, target = coef_out.at[side], coef_in.at[side]
        elif part == 1:
            source, target = half_out.at[side], half_in.at[side]
        else:
            source, target = rows_out.at[part - 2, side], rows_in.at[part - 2, side]
        return pltpu.make_async_remote_copy(
            src_ref=source,
            dst_ref=target,
            send_sem=move_send.at[side, part],
            recv_sem=move_recv.at[side, part],
            device_id=(place + 2 * side - 1, group),
            device_id_type=MESH,
        )

    def move_start(part):
        @pl.when(has_left)
        def _():
            move(0, part).start()

        @pl.when(has_right)
        def _():
            move(1, part).start()

    outer = [0, tiles - 1]
    inner = list(range(1, tiles - 1))
    move_start(0)
    load(0).wait()
    for side, slot in ((0, 0), (1, right_slot)):
        for t in range(tiles):
            rows = slice(t * TILE, (t + 1) * TILE)
            half_out[side, :, rows, :] = thin(spread(held_sol[slot, rows, :]), 1)
    move_start(1)
    load(1).wait()
    for side, slot in ((0, 0), (1, right_slot)):
        for part, which in ((0, outer), (1, inner)):
            for i, t in enumerate(which):
                rows_out[part, side, i] = held_rhs[slot, t * TILE : (t + 1) * TILE, :]

    def move_wait(part):
        @pl.when(has_right)
        def _():
            move(0, part).wait_recv()

        @pl.when(has_left)
        def _():
            move(1, part).wait_recv()

    def moved(field, b, t, arrived):
        rows = slice(t * TILE, (t + 1) * TILE)
        block = spread(held[field][own_slots[b], rows, :])
        if b == 0:
            block = jnp.where(first + b < start, arrived(1, rows), block)
        if b == boxes - 1:
            block = jnp.where(first + b >= end, arrived(0, rows), block)
        return block

    def face_to(k, side):
        return pltpu.make_async_remote_copy(
            src_ref=face_out.at[k, side],
            dst_ref=face_in.at[k, side],
            send_sem=face_send.at[k, side],
            recv_sem=face_recv.at[k, side],
            device_id=(place + 2 * side - 1, group),
            device_id_type=MESH,
        )

    def faces_start(k, plane_of):
        for b in range(boxes):
            for side in range(2):
                face_out[k, side, b] = plane_of(b, side)

        @pl.when(has_left)
        def _():
            face_to(k, 0).start()

        @pl.when(has_right)
        def _():
            face_to(k, 1).start()

    def faces_wait(k):
        @pl.when(has_left)
        def _():
            face_to(k, 1).wait_recv()

        @pl.when(has_right)
        def _():
            face_to(k, 0).wait_recv()

    def own_planes(ref):
        return lambda b, side: ref[
            b, :, PAD + side * (edge - 1) : PAD + side * (edge - 1) + 1, :
        ]

    links = [[link_ref[0, b, f] for f in range(FACES)] for b in range(boxes)]
    linked = [[jnp.where(t >= 0, 1.0, 0.0) for t in row] for row in links]
    beside = [[jnp.clip(t - first, 0, boxes - 1) for t in row] for row in links]

    def arrived_plane(k, b, f, plane):
        base = first + (2 * f - 1) * boxes
        for other in range(boxes):
            plane = jnp.where(
                (links[b][f] >= 0) & (links[b][f] == base + other),
                face_in[k, 1 - f, other],
                plane,
            )
        return plane

    no_plane = jnp.zeros((columns, 1, LANES), jnp.float32)
    ghost_at = (PAD - 1, PAD + edge)

    def ghost_rows(k, ref, keep_own):
        for b in range(boxes):
            for f in range(2):
                plane = own_planes(ref)(b, f) if keep_own else no_plane
                ref[b, :, ghost_at[f] : ghost_at[f] + 1, :] = arrived_plane(k, b, f, plane)

    def advance_ghosts(colour):
        for b in range(boxes):
            for f in range(2):
                row = slice(ghost_at[f], ghost_at[f] + 1)
                plane = sol[b, :, row, :]
                sol[b, :, row, :] = jnp.where(
                    ((plane_parity + 1 - f) & 1) == colour,
                    plane + arrived_plane(2, b, f, no_plane) * own_planes(sol)(b, f),
                    plane,
                )

    def around(ref, b, t):
        rows = slice(PAD + t * TILE, PAD + (t + 1) * TILE)
        here = ref[b, :, rows, :]
        low_y = pltpu.roll(here, edge, 2)
        high_y = pltpu.roll(here, LANES - edge, 2)
        ghost_low = pltpu.roll(ref[beside[b][2], columns - 1, rows, :], edge, 1)
        ghost_high = pltpu.roll(ref[beside[b][3], 0, rows, :], LANES - edge, 1)
        before = jnp.concatenate([ghost_low[None], low_y[:-1]], axis=0)
        after = jnp.concatenate([high_y[1:], ghost_high[None]], axis=0)
        return here, (
            ref[b, :, PAD + t * TILE - 1 : PAD + (t + 1) * TILE - 1, :],
            ref[b, :, PAD + t * TILE + 1 : PAD + (t + 1) * TILE + 1, :],
            jnp.where(low_lane, before, low_y),
            jnp.where(high_lane, after, high_y),
            jnp.where(
                low_depth,
                pltpu.roll(ref[beside[b][4], :, rows, :], LANES - edge + 1, 2),
                pltpu.roll(here, 1, 2),
            ),
            jnp.where(
                high_depth,
                pltpu.roll(ref[beside[b][5], :, rows, :], edge - 1, 2),
                pltpu.roll(here, LANES - 1, 2),
            ),
        )

    target = lax.broadcasted_iota(jnp.int32, merge_map.shape, 0)
    target = ((target >> edge.bit_length()) * half) + (
        (target & (edge - 1)) >> 1
    )
    merge_map[...] = jnp.where(
        target == lax.broadcasted_iota(jnp.int32, merge_map.shape, 1), 1.0, 0.0
    ).astype(jnp.bfloat16)
    for b in range(boxes):
        label = (
            parent_ref[0, b, 0] * coarse_slots + parent_ref[0, b, 1] * 8 + parent_ref[0, b, 2]
        ).astype(jnp.float32)
        pack[b, half : half + TILE, :] = jnp.full((TILE, half * half), label, jnp.float32)

    move_wait(0)
    for b in range(boxes):
        for t in range(tiles):
            coef[b, :, PAD + t * TILE : PAD + (t + 1) * TILE, :] = moved(
                2, b, t, lambda side, rows: spread(coef_in[side, rows, :])
            )
    faces_start(0, own_planes(coef))
    move_start(2)
    move_wait(1)
    for b in range(boxes):
        for t in range(tiles):
            sol[b, :, PAD + t * TILE : PAD + (t + 1) * TILE, :] = moved(
                0, b, t, lambda side, rows: thicken(half_in[side, :, rows, :])
            )
    faces_start(1, own_planes(sol))
    move_start(3)
    faces_wait(0)
    ghost_rows(0, coef, True)
    for b in range(boxes):
        for t in range(tiles):
            here, near = around(coef, b, t)
            total = jnp.full(shape, MASS_TERM, jnp.float32)
            kept = []
            for f in range(FACES):
                beyond = near[f]
                if f >= 2:
                    inside = linked[b][f]
                    beyond = jnp.where(
                        edge_masks[f], beyond * inside + here * (1.0 - inside), beyond
                    )
                weight = 0.5 * (here + beyond)
                total = total + weight
                if f >= 2:
                    weight = jnp.where(edge_masks[f], weight * linked[b][f], weight)
                kept.append(weight)
            over = 1.0 / total
            diagonal[b, t] = total
            inverse[b, t] = over
            for f in range(FACES):
                weights[b, t, f] = kept[f] * over

    faces_start(
        2,
        lambda b, side: weights[
            b, side * (tiles - 1), side, :, side * (TILE - 1) : side * (TILE - 1) + 1, :
        ],
    )

    def scale_rhs(part, which):
        move_wait(part)
        for b in range(boxes):
            for i, t in enumerate(which):
                scaled_rhs[b, t] = inverse[b, t] * moved(
                    1, b, t, lambda side, rows, i=i: spread(rows_in[part - 2, side, i])
                )

    def relaxed(b, t):
        here, near = around(sol, b, t)
        total = scaled_rhs[b, t]
        for f in range(FACES):
            total = total + weights[b, t, f] * near[f]
        return here, total

    def sweep(colour, which):
        for b in range(boxes):
            for t in which:
                here, total = relaxed(b, t)
                sol[b, :, PAD + t * TILE : PAD + (t + 1) * TILE, :] = jnp.where(
                    parity == colour, total, here
                )

    def next_planes(colour):
        def plane_of(b, side):
            t = side * (tiles - 1)
            here, near = around(sol, b, t)
            total = scaled_rhs[b, t]
            for f in range(FACES):
                if f != side:
                    total = total + weights[b, t, f] * near[f]
            block = jnp.where(parity == colour, total, here)
            return block[:, side * (TILE - 1) : side * (TILE - 1) + 1, :]

        return plane_of

    faces_wait(1)
    ghost_rows(1, sol, False)
    scale_rhs(2, outer)
    sweep(0, outer)
    faces_start(3, next_planes(1))
    scale_rhs(3, inner)
    sweep(0, inner)
    sweep(1, inner)
    faces_wait(2)
    faces_wait(3)
    ghost_rows(3, sol, False)
    sweep(1, outer)
    advance_ghosts(1)
    sweep(0, outer)
    faces_start(4, next_planes(1))
    sweep(0, inner)
    sweep(1, inner)
    faces_wait(4)
    ghost_rows(4, sol, False)
    sweep(1, outer)
    advance_ghosts(1)

    def leave(which):
        for b in range(boxes):
            for t in which:
                here, total = relaxed(b, t)
                res_rows[b, t * TILE : (t + 1) * TILE, :] = flatten(
                    diagonal[b, t] * (total - here)
                )

    leave(range(tiles))
    residual_store = pltpu.make_async_copy(res_rows, residual_out.at[0], store_sem.at[1])
    residual_store.start()

    for b in range(boxes):
        rows = res_rows[b]
        high = rows.astype(jnp.bfloat16)
        low = (rows - high.astype(jnp.float32)).astype(jnp.bfloat16)
        both = jnp.dot(
            jnp.concatenate([high, low], axis=0),
            merge_map[...],
            preferred_element_type=jnp.float32,
        )
        both = both[:edge] + both[edge:]
        for c in range(merged.shape[1]):
            merged[b, c] = both[:, c * LANES : (c + 1) * LANES]
    for b in range(boxes):
        for c in range(merged.shape[1]):
            pack[b, 0:half, c * LANES : (c + 1) * LANES] = 0.125 * (
                merged[b, c, pl.ds(0, half, stride=2), :]
                + merged[b, c, pl.ds(1, half, stride=2), :]
            )

    def pack_to(step):
        return pltpu.make_async_remote_copy(
            src_ref=pack,
            dst_ref=packs_out.at[step],
            send_sem=pack_send.at[step - 1],
            recv_sem=pack_recv.at[step - 1],
            device_id=(place, lax.rem(group + step, groups)),
            device_id_type=MESH,
        )

    for step in range(1, groups):
        pack_to(step).start()
    for b in range(boxes):
        for t in range(tiles):
            plane_out[b, t * TILE : (t + 1) * TILE, :] = flatten(
                sol[b, :, PAD + t * TILE : PAD + (t + 1) * TILE, :]
            )
    smooth_store = pltpu.make_async_copy(plane_out, smooth_out.at[0], store_sem.at[0])
    smooth_store.start()
    own_store = pltpu.make_async_copy(pack, packs_out.at[0], store_sem.at[2])
    own_store.start()
    for step in range(1, groups):
        pack_to(step).wait_recv()

    for step in range(1, groups):
        pack_to(step).wait_send()

    @pl.when(has_left)
    def _():
        for part in range(4):
            move(0, part).wait_send()
        for k in range(5):
            face_to(k, 0).wait_send()

    @pl.when(has_right)
    def _():
        for part in range(4):
            move(1, part).wait_send()
        for k in range(5):
            face_to(k, 1).wait_send()

    smooth_store.wait()
    residual_store.wait()
    own_store.wait()


def hand_out_kernel(
    smooth_in,
    residual_in,
    packs_in,
    coarse_in,
    smooth_out,
    residual_out,
    coarse_out,
    smooth_buf,
    residual_buf,
    packs,
    coarse,
    load_sem,
    store_sem,
):
    group = lax.axis_index("grp")
    groups, boxes = packs.shape[:2]
    slots, half = coarse.shape[:2]
    loads = [
        pltpu.make_async_copy(source, target, load_sem.at[i])
        for i, (source, target) in enumerate(
            (
                (packs_in, packs),
                (coarse_in, coarse),
                (smooth_in, smooth_buf),
                (residual_in, residual_buf),
            )
        )
    ]
    stores = [
        pltpu.make_async_copy(source, target, store_sem.at[i])
        for i, (source, target) in enumerate(
            ((smooth_buf, smooth_out), (residual_buf, residual_out), (coarse, coarse_out))
        )
    ]
    for load in loads:
        load.start()
    for load in loads:
        load.wait()
    stores[0].start()
    stores[1].start()
    for source in range(groups):
        for b in range(boxes):
            label = packs[source, b, half : half + TILE, :]
            label = jnp.concatenate([label] * (half // TILE), axis=0)
            values = packs[source, b, 0:half, :]
            for s in range(slots):
                mine = (group * slots + s).astype(jnp.float32)
                coarse[s] = jnp.where(label == mine, values, coarse[s])
    stores[2].start()
    for store in stores:
        store.wait()


def per_device(old_fields, old_count, neighbours, parents, coarse_source):
    _, _, slots, edge, cells = old_fields.shape
    boxes = neighbours.shape[1]
    groups = lax.axis_size("grp")
    _, coarse_boxes, octants, half, quarter = coarse_source.shape
    tiles = edge // TILE
    columns = cells // LANES
    padded = edge + 2 * PAD
    f32 = jnp.float32
    coarse_slots = coarse_boxes * octants
    scratch = [
        pltpu.SMEM(old_count.shape, jnp.int32),
        pltpu.SMEM(neighbours.shape, jnp.int32),
        pltpu.SMEM(parents.shape, jnp.int32),
        pltpu.VMEM((slots, edge, cells), f32),
        pltpu.VMEM((slots, edge, cells), f32),
        pltpu.VMEM((slots, edge, cells), f32),
        pltpu.VMEM((2, edge, cells), f32),
        pltpu.VMEM((2, edge, cells), f32),
        pltpu.VMEM((2, columns // 2, edge, LANES), f32),
        pltpu.VMEM((2, columns // 2, edge, LANES), f32),
        pltpu.VMEM((2, 2, tiles // 2, TILE, cells), f32),
        pltpu.VMEM((2, 2, tiles // 2, TILE, cells), f32),
        pltpu.VMEM((boxes, columns, padded, LANES), f32),
        pltpu.VMEM((boxes, columns, padded, LANES), f32),
        pltpu.VMEM((boxes, tiles, FACES, columns, TILE, LANES), f32),
        pltpu.VMEM((boxes, tiles, columns, TILE, LANES), f32),
        pltpu.VMEM((boxes, tiles, columns, TILE, LANES), f32),
        pltpu.VMEM((boxes, tiles, columns, TILE, LANES), f32),
        pltpu.VMEM((boxes, edge, cells), f32),
        pltpu.VMEM((boxes, edge, cells), f32),
        pltpu.VMEM((cells, quarter), jnp.bfloat16),
        pltpu.VMEM((boxes, quarter // LANES, edge, LANES), f32),
        pltpu.VMEM((boxes, half + TILE, quarter), f32),
        pltpu.VMEM((5, 2, boxes, columns, 1, LANES), f32),
        pltpu.VMEM((5, 2, boxes, columns, 1, LANES), f32),
        pltpu.SemaphoreType.DMA((6,)),
        pltpu.SemaphoreType.DMA((2, 4)),
        pltpu.SemaphoreType.DMA((2, 4)),
        pltpu.SemaphoreType.DMA((5, 2)),
        pltpu.SemaphoreType.DMA((5, 2)),
        pltpu.SemaphoreType.DMA((groups - 1,)),
        pltpu.SemaphoreType.DMA((groups - 1,)),
        pltpu.SemaphoreType.DMA((3,)),
    ]
    anywhere = pl.BlockSpec(memory_space=pl.ANY)
    in_hbm = pl.BlockSpec(memory_space=pltpu.HBM)
    smoothed, residual, packs = pl.pallas_call(
        functools.partial(level_kernel, coarse_slots),
        out_shape=(
            jax.ShapeDtypeStruct((1, boxes, edge, cells), f32),
            jax.ShapeDtypeStruct((1, boxes, edge, cells), f32),
            jax.ShapeDtypeStruct((groups, boxes, half + TILE, quarter), f32),
        ),
        in_specs=[in_hbm] * 4,
        out_specs=(anywhere, anywhere, anywhere),
        scratch_shapes=scratch,
        compiler_params=pltpu.CompilerParams(
            collective_id=0, has_side_effects=True, vmem_limit_bytes=VMEM_BYTES
        ),
    )(
        old_fields,
        old_count,
        neighbours,
        parents,
    )
    coarse = coarse_source.reshape(coarse_slots, half, quarter)
    parts = (smoothed, residual, packs, coarse)
    results = (smoothed, residual, coarse)
    smoothed, residual, coarse_rhs = pl.pallas_call(
        hand_out_kernel,
        out_shape=tuple(jax.ShapeDtypeStruct(part.shape, f32) for part in results),
        in_specs=[in_hbm] * 4,
        out_specs=(in_hbm,) * 3,
        scratch_shapes=[pltpu.VMEM(part.shape, f32) for part in parts]
        + [pltpu.SemaphoreType.DMA((4,)), pltpu.SemaphoreType.DMA((3,))],
        compiler_params=pltpu.CompilerParams(vmem_limit_bytes=VMEM_BYTES),
    )(*parts)
    return smoothed, residual, coarse_rhs.reshape(coarse_source.shape)


def solution(mesh):
    in_specs = (
        P(None, "grp", "box", None, None),
        P("grp", None),
        P("grp", "box", None),
        P("grp", "box", None),
        P("grp", "box", None, None, None),
    )
    out_specs = (
        P("grp", "box", None, None),
        P("grp", "box", None, None),
        P("grp", "box", None, None, None),
    )
    return jax.shard_map(
        per_device, mesh=mesh, in_specs=in_specs, out_specs=out_specs, check_vma=False
    )
```

```python
import functools

import jax
import jax.numpy as jnp
from jax import lax
from jax.experimental import pallas as pl
from jax.experimental.pallas import tpu as pltpu
from jax.sharding import PartitionSpec as P

MASS_TERM = 0.25
MESH = pl.DeviceIdType.MESH
LANES = 128
TILE = 8
PAD = 8
FACES = 6
VMEM_BYTES = 60 * 1024 * 1024


def level_kernel(
    coarse_slots,
    old_ref,
    count_hbm,
    link_hbm,
    parent_hbm,
    smooth_out,
    residual_out,
    packs_out,
    count_ref,
    link_ref,
    parent_ref,
    held_sol,
    held_rhs,
    held_coef,
    coef_out,
    coef_in,
    half_out,
    half_in,
    rows_out,
    rows_in,
    sol,
    coef,
    weights,
    diagonal,
    inverse,
    scaled_rhs,
    plane_out,
    res_rows,
    merge_map,
    merged,
    pack,
    face_out,
    face_in,
    load_sem,
    move_send,
    move_recv,
    face_send,
    face_recv,
    pack_send,
    pack_recv,
    store_sem,
):
    place = lax.axis_index("box")
    group = lax.axis_index("grp")
    curve = lax.axis_size("box")
    groups = lax.axis_size("grp")
    slots = old_ref.shape[2]
    boxes = link_ref.shape[1]
    edge = old_ref.shape[3]
    cells = old_ref.shape[4]
    tiles = edge // TILE
    columns = cells // LANES
    half = edge // 2
    has_left = place > 0
    has_right = place < curve - 1
    held = (held_sol, held_rhs, held_coef)

    def load(field):
        return pltpu.make_async_copy(old_ref.at[field, 0], held[field], load_sem.at[field])

    tables = [
        pltpu.make_async_copy(source, target, load_sem.at[3 + i])
        for i, (source, target) in enumerate(
            ((count_hbm, count_ref), (link_hbm, link_ref), (parent_hbm, parent_ref))
        )
    ]
    barrier = pltpu.get_barrier_semaphore()

    @pl.when(has_left)
    def _():
        pl.semaphore_signal(barrier, inc=1, device_id=(place - 1, group), device_id_type=MESH)

    @pl.when(has_right)
    def _():
        pl.semaphore_signal(barrier, inc=1, device_id=(place + 1, group), device_id_type=MESH)

    for step in range(1, groups):
        pl.semaphore_signal(
            barrier,
            inc=1,
            device_id=(place, lax.rem(group + step, groups)),
            device_id_type=MESH,
        )
    for table in tables:
        table.start()
    for field in (2, 0, 1):
        load(field).start()

    shape = (columns, TILE, LANES)
    lane = lax.broadcasted_iota(jnp.int32, shape, 2)
    column = lax.broadcasted_iota(jnp.int32, shape, 0)
    depth = lane & (edge - 1)
    low_depth = depth == 0
    high_depth = depth == edge - 1
    low_lane = lane < edge
    high_lane = lane >= LANES - edge
    low_row = low_lane & (column == 0)
    high_row = high_lane & (column == columns - 1)
    edge_masks = (None, None, low_row, high_row, low_depth, high_depth)
    parity = (
        lax.broadcasted_iota(jnp.int32, shape, 1)
        + column * (LANES // edge)
        + (lane >> (edge.bit_length() - 1))
        + depth
    ) & 1
    plane_shape = (columns, 1, LANES)
    plane_lane = lax.broadcasted_iota(jnp.int32, plane_shape, 2)
    plane_parity = (
        lax.broadcasted_iota(jnp.int32, plane_shape, 0) * (LANES // edge)
        + (plane_lane >> (edge.bit_length() - 1))
        + (plane_lane & (edge - 1))
    ) & 1
    pairs = columns // 2
    even_line = ((lane[:pairs] >> (edge.bit_length() - 1)) & 1) == 0
    odd_cell = parity[:pairs] == 1

    def spread(rows):
        return jnp.stack([rows[:, c * LANES : (c + 1) * LANES] for c in range(columns)])

    def flatten(block):
        return jnp.concatenate([block[c] for c in range(columns)], axis=1)

    def thin(block, colour):
        low, high = block[:pairs], block[pairs:]
        low_next = pltpu.roll(low, LANES - edge, 2)
        high_next = pltpu.roll(high, edge, 2)
        if colour:
            low = jnp.where(odd_cell, low, low_next)
            high = jnp.where(odd_cell, high, high_next)
        else:
            low = jnp.where(odd_cell, low_next, low)
            high = jnp.where(odd_cell, high_next, high)
        return jnp.where(even_line, low, high)

    def thicken(block):
        low = jnp.where(even_line, block, pltpu.roll(block, edge, 2))
        high = jnp.where(even_line, pltpu.roll(block, LANES - edge, 2), block)
        return jnp.concatenate([low, high], axis=0)

    for table in tables:
        table.wait()
    start = jnp.int32(0)
    for other in range(curve):
        start = start + jnp.where(other < place, count_ref[0, other], 0)
    end = start
    for other in range(curve):
        end = end + jnp.where(other == place, count_ref[0, other], 0)
    first = place * boxes
    right_slot = jnp.clip(first + boxes - start, 0, slots - 1)
    own_slots = [jnp.clip(first + b - start, 0, slots - 1) for b in range(boxes)]
    load(2).wait()
    for side, slot in ((0, 0), (1, right_slot)):
        coef_out[side] = held_coef[slot]
    pl.semaphore_wait(
        barrier, groups - 1 + has_left.astype(jnp.int32) + has_right.astype(jnp.int32)
    )

    def move(side, part):
        if part == 0:
            source, target = coef_out.at[side], coef_in.at[side]
        elif part == 1:
            source, target = half_out.at[side], half_in.at[side]
        else:
            source, target = rows_out.at[part - 2, side], rows_in.at[part - 2, side]
        return pltpu.make_async_remote_copy(
            src_ref=source,
            dst_ref=target,
            send_sem=move_send.at[side, part],
            recv_sem=move_recv.at[side, part],
            device_id=(place + 2 * side - 1, group),
            device_id_type=MESH,
        )

    def move_start(part):
        @pl.when(has_left)
        def _():
            move(0, part).start()

        @pl.when(has_right)
        def _():
            move(1, part).start()

    outer = [0, tiles - 1]
    inner = list(range(1, tiles - 1))
    move_start(0)
    load(0).wait()
    for side, slot in ((0, 0), (1, right_slot)):
        for t in range(tiles):
            rows = slice(t * TILE, (t + 1) * TILE)
            half_out[side, :, rows, :] = thin(spread(held_sol[slot, rows, :]), 1)
    move_start(1)
    load(1).wait()
    for side, slot in ((0, 0), (1, right_slot)):
        for part, which in ((0, outer), (1, inner)):
            for i, t in enumerate(which):
                rows_out[part, side, i] = held_rhs[slot, t * TILE : (t + 1) * TILE, :]
    move_start(2)

    def move_wait(part):
        @pl.when(has_right)
        def _():
            move(0, part).wait_recv()

        @pl.when(has_left)
        def _():
            move(1, part).wait_recv()

    def moved(field, b, t, arrived):
        rows = slice(t * TILE, (t + 1) * TILE)
        block = spread(held[field][own_slots[b], rows, :])
        if b == 0:
            block = jnp.where(first + b < start, arrived(1, rows), block)
        if b == boxes - 1:
            block = jnp.where(first + b >= end, arrived(0, rows), block)
        return block

    def face_to(k, side):
        return pltpu.make_async_remote_copy(
            src_ref=face_out.at[k, side],
            dst_ref=face_in.at[k, side],
            send_sem=face_send.at[k, side],
            recv_sem=face_recv.at[k, side],
            device_id=(place + 2 * side - 1, group),
            device_id_type=MESH,
        )

    def faces_start(k, plane_of):
        for b in range(boxes):
            for side in range(2):
                face_out[k, side, b] = plane_of(b, side)

        @pl.when(has_left)
        def _():
            face_to(k, 0).start()

        @pl.when(has_right)
        def _():
            face_to(k, 1).start()

    def faces_wait(k):
        @pl.when(has_left)
        def _():
            face_to(k, 1).wait_recv()

        @pl.when(has_right)
        def _():
            face_to(k, 0).wait_recv()

    def own_planes(ref):
        return lambda b, side: ref[
            b, :, PAD + side * (edge - 1) : PAD + side * (edge - 1) + 1, :
        ]

    links = [[link_ref[0, b, f] for f in range(FACES)] for b in range(boxes)]
    linked = [[jnp.where(t >= 0, 1.0, 0.0) for t in row] for row in links]
    beside = [[jnp.clip(t - first, 0, boxes - 1) for t in row] for row in links]

    def arrived_plane(k, b, f, plane):
        base = first + (2 * f - 1) * boxes
        for other in range(boxes):
            plane = jnp.where(
                (links[b][f] >= 0) & (links[b][f] == base + other),
                face_in[k, 1 - f, other],
                plane,
            )
        return plane

    no_plane = jnp.zeros((columns, 1, LANES), jnp.float32)
    ghost_at = (PAD - 1, PAD + edge)

    def ghost_rows(k, ref, keep_own):
        for b in range(boxes):
            for f in range(2):
                plane = own_planes(ref)(b, f) if keep_own else no_plane
                ref[b, :, ghost_at[f] : ghost_at[f] + 1, :] = arrived_plane(k, b, f, plane)

    def advance_ghosts(colour):
        for b in range(boxes):
            for f in range(2):
                row = slice(ghost_at[f], ghost_at[f] + 1)
                plane = sol[b, :, row, :]
                sol[b, :, row, :] = jnp.where(
                    ((plane_parity + 1 - f) & 1) == colour,
                    plane + arrived_plane(2, b, f, no_plane) * own_planes(sol)(b, f),
                    plane,
                )

    def around(ref, b, t):
        rows = slice(PAD + t * TILE, PAD + (t + 1) * TILE)
        here = ref[b, :, rows, :]
        low_y = pltpu.roll(here, edge, 2)
        high_y = pltpu.roll(here, LANES - edge, 2)
        ghost_low = pltpu.roll(ref[beside[b][2], columns - 1, rows, :], edge, 1)
        ghost_high = pltpu.roll(ref[beside[b][3], 0, rows, :], LANES - edge, 1)
        before = jnp.concatenate([ghost_low[None], low_y[:-1]], axis=0)
        after = jnp.concatenate([high_y[1:], ghost_high[None]], axis=0)
        return here, (
            ref[b, :, PAD + t * TILE - 1 : PAD + (t + 1) * TILE - 1, :],
            ref[b, :, PAD + t * TILE + 1 : PAD + (t + 1) * TILE + 1, :],
            jnp.where(low_lane, before, low_y),
            jnp.where(high_lane, after, high_y),
            jnp.where(
                low_depth,
                pltpu.roll(ref[beside[b][4], :, rows, :], LANES - edge + 1, 2),
                pltpu.roll(here, 1, 2),
            ),
            jnp.where(
                high_depth,
                pltpu.roll(ref[beside[b][5], :, rows, :], edge - 1, 2),
                pltpu.roll(here, LANES - 1, 2),
            ),
        )

    target = lax.broadcasted_iota(jnp.int32, merge_map.shape, 0)
    target = ((target >> edge.bit_length()) * half) + (
        (target & (edge - 1)) >> 1
    )
    merge_map[...] = jnp.where(
        target == lax.broadcasted_iota(jnp.int32, merge_map.shape, 1), 1.0, 0.0
    ).astype(jnp.bfloat16)
    for b in range(boxes):
        label = (
            parent_ref[0, b, 0] * coarse_slots + parent_ref[0, b, 1] * 8 + parent_ref[0, b, 2]
        ).astype(jnp.float32)
        pack[b, half : half + TILE, :] = jnp.full((TILE, half * half), label, jnp.float32)

    move_wait(0)
    for b in range(boxes):
        for t in range(tiles):
            coef[b, :, PAD + t * TILE : PAD + (t + 1) * TILE, :] = moved(
                2, b, t, lambda side, rows: spread(coef_in[side, rows, :])
            )
    faces_start(0, own_planes(coef))
    move_wait(1)
    for b in range(boxes):
        for t in range(tiles):
            sol[b, :, PAD + t * TILE : PAD + (t + 1) * TILE, :] = moved(
                0, b, t, lambda side, rows: thicken(half_in[side, :, rows, :])
            )
    faces_start(1, own_planes(sol))
    move_start(3)
    faces_wait(0)
    ghost_rows(0, coef, True)
    for b in range(boxes):
        for t in range(tiles):
            here, near = around(coef, b, t)
            total = jnp.full(shape, MASS_TERM, jnp.float32)
            kept = []
            for f in range(FACES):
                beyond = near[f]
                if f >= 2:
                    inside = linked[b][f]
                    beyond = jnp.where(
                        edge_masks[f], beyond * inside + here * (1.0 - inside), beyond
                    )
                weight = 0.5 * (here + beyond)
                total = total + weight
                if f >= 2:
                    weight = jnp.where(edge_masks[f], weight * linked[b][f], weight)
                kept.append(weight)
            over = 1.0 / total
            diagonal[b, t] = total
            inverse[b, t] = over
            for f in range(FACES):
                weights[b, t, f] = kept[f] * over

    faces_start(
        2,
        lambda b, side: weights[
            b, side * (tiles - 1), side, :, side * (TILE - 1) : side * (TILE - 1) + 1, :
        ],
    )

    def scale_rhs(part, which):
        move_wait(part)
        for b in range(boxes):
            for i, t in enumerate(which):
                scaled_rhs[b, t] = inverse[b, t] * moved(
                    1, b, t, lambda side, rows, i=i: spread(rows_in[part - 2, side, i])
                )

    def relaxed(b, t):
        here, near = around(sol, b, t)
        total = scaled_rhs[b, t]
        for f in range(FACES):
            total = total + weights[b, t, f] * near[f]
        return here, total

    def sweep(colour, which):
        for b in range(boxes):
            for t in which:
                here, total = relaxed(b, t)
                sol[b, :, PAD + t * TILE : PAD + (t + 1) * TILE, :] = jnp.where(
                    parity == colour, total, here
                )

    def next_planes(colour):
        def plane_of(b, side):
            t = side * (tiles - 1)
            here, near = around(sol, b, t)
            total = scaled_rhs[b, t]
            for f in range(FACES):
                if f != side:
                    total = total + weights[b, t, f] * near[f]
            block = jnp.where(parity == colour, total, here)
            return block[:, side * (TILE - 1) : side * (TILE - 1) + 1, :]

        return plane_of

    faces_wait(1)
    ghost_rows(1, sol, False)
    scale_rhs(2, outer)
    sweep(0, outer)
    faces_start(3, next_planes(1))
    scale_rhs(3, inner)
    sweep(0, inner)
    sweep(1, inner)
    faces_wait(2)
    faces_wait(3)
    ghost_rows(3, sol, False)
    sweep(1, outer)
    advance_ghosts(1)
    sweep(0, outer)
    faces_start(4, next_planes(1))
    sweep(0, inner)
    sweep(1, inner)
    faces_wait(4)
    ghost_rows(4, sol, False)
    sweep(1, outer)
    advance_ghosts(1)

    def leave(which):
        for b in range(boxes):
            for t in which:
                here, total = relaxed(b, t)
                res_rows[b, t * TILE : (t + 1) * TILE, :] = flatten(
                    diagonal[b, t] * (total - here)
                )

    leave(range(tiles))
    residual_store = pltpu.make_async_copy(res_rows, residual_out.at[0], store_sem.at[1])
    residual_store.start()

    for b in range(boxes):
        rows = res_rows[b]
        high = rows.astype(jnp.bfloat16)
        low = (rows - high.astype(jnp.float32)).astype(jnp.bfloat16)
        both = jnp.dot(
            jnp.concatenate([high, low], axis=0),
            merge_map[...],
            preferred_element_type=jnp.float32,
        )
        both = both[:edge] + both[edge:]
        for c in range(merged.shape[1]):
            merged[b, c] = both[:, c * LANES : (c + 1) * LANES]
    for b in range(boxes):
        for c in range(merged.shape[1]):
            pack[b, 0:half, c * LANES : (c + 1) * LANES] = 0.125 * (
                merged[b, c, pl.ds(0, half, stride=2), :]
                + merged[b, c, pl.ds(1, half, stride=2), :]
            )

    def pack_to(step):
        return pltpu.make_async_remote_copy(
            src_ref=pack,
            dst_ref=packs_out.at[step],
            send_sem=pack_send.at[step - 1],
            recv_sem=pack_recv.at[step - 1],
            device_id=(place, lax.rem(group + step, groups)),
            device_id_type=MESH,
        )

    for step in range(1, groups):
        pack_to(step).start()
    for b in range(boxes):
        for t in range(tiles):
            plane_out[b, t * TILE : (t + 1) * TILE, :] = flatten(
                sol[b, :, PAD + t * TILE : PAD + (t + 1) * TILE, :]
            )
    smooth_store = pltpu.make_async_copy(plane_out, smooth_out.at[0], store_sem.at[0])
    smooth_store.start()
    own_store = pltpu.make_async_copy(pack, packs_out.at[0], store_sem.at[2])
    own_store.start()
    for step in range(1, groups):
        pack_to(step).wait_recv()

    for step in range(1, groups):
        pack_to(step).wait_send()

    @pl.when(has_left)
    def _():
        for part in range(4):
            move(0, part).wait_send()
        for k in range(5):
            face_to(k, 0).wait_send()

    @pl.when(has_right)
    def _():
        for part in range(4):
            move(1, part).wait_send()
        for k in range(5):
            face_to(k, 1).wait_send()

    smooth_store.wait()
    residual_store.wait()
    own_store.wait()


def hand_out_kernel(
    smooth_in,
    residual_in,
    packs_in,
    coarse_in,
    smooth_out,
    residual_out,
    coarse_out,
    smooth_buf,
    residual_buf,
    packs,
    coarse,
    load_sem,
    store_sem,
):
    group = lax.axis_index("grp")
    groups, boxes = packs.shape[:2]
    slots, half = coarse.shape[:2]
    loads = [
        pltpu.make_async_copy(source, target, load_sem.at[i])
        for i, (source, target) in enumerate(
            (
                (packs_in, packs),
                (coarse_in, coarse),
                (smooth_in, smooth_buf),
                (residual_in, residual_buf),
            )
        )
    ]
    stores = [
        pltpu.make_async_copy(source, target, store_sem.at[i])
        for i, (source, target) in enumerate(
            ((smooth_buf, smooth_out), (residual_buf, residual_out), (coarse, coarse_out))
        )
    ]
    for load in loads:
        load.start()
    loads[0].wait()
    loads[1].wait()
    for source in range(groups):
        for b in range(boxes):
            label = packs[source, b, half : half + TILE, :]
            label = jnp.concatenate([label] * (half // TILE), axis=0)
            values = packs[source, b, 0:half, :]
            for s in range(slots):
                mine = (group * slots + s).astype(jnp.float32)
                coarse[s] = jnp.where(label == mine, values, coarse[s])
    stores[2].start()
    for i in range(2):
        loads[2 + i].wait()
        stores[i].start()
    for store in stores:
        store.wait()


def per_device(old_fields, old_count, neighbours, parents, coarse_source):
    _, _, slots, edge, cells = old_fields.shape
    boxes = neighbours.shape[1]
    groups = lax.axis_size("grp")
    _, coarse_boxes, octants, half, quarter = coarse_source.shape
    tiles = edge // TILE
    columns = cells // LANES
    padded = edge + 2 * PAD
    f32 = jnp.float32
    coarse_slots = coarse_boxes * octants
    scratch = [
        pltpu.SMEM(old_count.shape, jnp.int32),
        pltpu.SMEM(neighbours.shape, jnp.int32),
        pltpu.SMEM(parents.shape, jnp.int32),
        pltpu.VMEM((slots, edge, cells), f32),
        pltpu.VMEM((slots, edge, cells), f32),
        pltpu.VMEM((slots, edge, cells), f32),
        pltpu.VMEM((2, edge, cells), f32),
        pltpu.VMEM((2, edge, cells), f32),
        pltpu.VMEM((2, columns // 2, edge, LANES), f32),
        pltpu.VMEM((2, columns // 2, edge, LANES), f32),
        pltpu.VMEM((2, 2, tiles // 2, TILE, cells), f32),
        pltpu.VMEM((2, 2, tiles // 2, TILE, cells), f32),
        pltpu.VMEM((boxes, columns, padded, LANES), f32),
        pltpu.VMEM((boxes, columns, padded, LANES), f32),
        pltpu.VMEM((boxes, tiles, FACES, columns, TILE, LANES), f32),
        pltpu.VMEM((boxes, tiles, columns, TILE, LANES), f32),
        pltpu.VMEM((boxes, tiles, columns, TILE, LANES), f32),
        pltpu.VMEM((boxes, tiles, columns, TILE, LANES), f32),
        pltpu.VMEM((boxes, edge, cells), f32),
        pltpu.VMEM((boxes, edge, cells), f32),
        pltpu.VMEM((cells, quarter), jnp.bfloat16),
        pltpu.VMEM((boxes, quarter // LANES, edge, LANES), f32),
        pltpu.VMEM((boxes, half + TILE, quarter), f32),
        pltpu.VMEM((5, 2, boxes, columns, 1, LANES), f32),
        pltpu.VMEM((5, 2, boxes, columns, 1, LANES), f32),
        pltpu.SemaphoreType.DMA((6,)),
        pltpu.SemaphoreType.DMA((2, 4)),
        pltpu.SemaphoreType.DMA((2, 4)),
        pltpu.SemaphoreType.DMA((5, 2)),
        pltpu.SemaphoreType.DMA((5, 2)),
        pltpu.SemaphoreType.DMA((groups - 1,)),
        pltpu.SemaphoreType.DMA((groups - 1,)),
        pltpu.SemaphoreType.DMA((3,)),
    ]
    anywhere = pl.BlockSpec(memory_space=pl.ANY)
    in_hbm = pl.BlockSpec(memory_space=pltpu.HBM)
    smoothed, residual, packs = pl.pallas_call(
        functools.partial(level_kernel, coarse_slots),
        out_shape=(
            jax.ShapeDtypeStruct((1, boxes, edge, cells), f32),
            jax.ShapeDtypeStruct((1, boxes, edge, cells), f32),
            jax.ShapeDtypeStruct((groups, boxes, half + TILE, quarter), f32),
        ),
        in_specs=[in_hbm] * 4,
        out_specs=(anywhere, anywhere, anywhere),
        scratch_shapes=scratch,
        compiler_params=pltpu.CompilerParams(
            collective_id=0, has_side_effects=True, vmem_limit_bytes=VMEM_BYTES
        ),
    )(
        old_fields,
        old_count,
        neighbours,
        parents,
    )
    coarse = coarse_source.reshape(coarse_slots, half, quarter)
    parts = (smoothed, residual, packs, coarse)
    results = (smoothed, residual, coarse)
    smoothed, residual, coarse_rhs = pl.pallas_call(
        hand_out_kernel,
        out_shape=tuple(jax.ShapeDtypeStruct(part.shape, f32) for part in results),
        in_specs=[in_hbm] * 4,
        out_specs=(in_hbm,) * 3,
        scratch_shapes=[pltpu.VMEM(part.shape, f32) for part in parts]
        + [pltpu.SemaphoreType.DMA((4,)), pltpu.SemaphoreType.DMA((3,))],
        compiler_params=pltpu.CompilerParams(vmem_limit_bytes=VMEM_BYTES),
    )(*parts)
    return smoothed, residual, coarse_rhs.reshape(coarse_source.shape)


def solution(mesh):
    in_specs = (
        P(None, "grp", "box", None, None),
        P("grp", None),
        P("grp", "box", None),
        P("grp", "box", None),
        P("grp", "box", None, None, None),
    )
    out_specs = (
        P("grp", "box", None, None),
        P("grp", "box", None, None),
        P("grp", "box", None, None, None),
    )
    return jax.shard_map(
        per_device, mesh=mesh, in_specs=in_specs, out_specs=out_specs, check_vma=False
    )
```

```python
import functools

import jax
import jax.numpy as jnp
from jax import lax
from jax.experimental import pallas as pl
from jax.experimental.pallas import tpu as pltpu
from jax.sharding import PartitionSpec as P

MASS_TERM = 0.25
MESH = pl.DeviceIdType.MESH
LANES = 128
TILE = 8
PAD = 8
FACES = 6
VMEM_BYTES = 60 * 1024 * 1024


def level_kernel(
    coarse_slots,
    old_ref,
    count_hbm,
    link_hbm,
    parent_hbm,
    smooth_out,
    residual_out,
    packs_out,
    count_ref,
    link_ref,
    parent_ref,
    held_sol,
    held_rhs,
    held_coef,
    coef_out,
    coef_in,
    half_out,
    half_in,
    rows_out,
    rows_in,
    sol,
    coef,
    weights,
    diagonal,
    inverse,
    scaled_rhs,
    plane_out,
    res_rows,
    merge_map,
    merged,
    pack,
    face_out,
    face_in,
    load_sem,
    move_send,
    move_recv,
    face_send,
    face_recv,
    pack_send,
    pack_recv,
    store_sem,
):
    place = lax.axis_index("box")
    group = lax.axis_index("grp")
    curve = lax.axis_size("box")
    groups = lax.axis_size("grp")
    slots = old_ref.shape[2]
    boxes = link_ref.shape[1]
    edge = old_ref.shape[3]
    cells = old_ref.shape[4]
    tiles = edge // TILE
    columns = cells // LANES
    half = edge // 2
    has_left = place > 0
    has_right = place < curve - 1
    held = (held_sol, held_rhs, held_coef)

    def load(field):
        return pltpu.make_async_copy(old_ref.at[field, 0], held[field], load_sem.at[field])

    tables = [
        pltpu.make_async_copy(source, target, load_sem.at[3 + i])
        for i, (source, target) in enumerate(
            ((count_hbm, count_ref), (link_hbm, link_ref), (parent_hbm, parent_ref))
        )
    ]
    barrier = pltpu.get_barrier_semaphore()

    @pl.when(has_left)
    def _():
        pl.semaphore_signal(barrier, inc=1, device_id=(place - 1, group), device_id_type=MESH)

    @pl.when(has_right)
    def _():
        pl.semaphore_signal(barrier, inc=1, device_id=(place + 1, group), device_id_type=MESH)

    for step in range(1, groups):
        pl.semaphore_signal(
            barrier,
            inc=1,
            device_id=(place, lax.rem(group + step, groups)),
            device_id_type=MESH,
        )
    for table in tables:
        table.start()
    for field in (2, 0, 1):
        load(field).start()

    shape = (columns, TILE, LANES)
    lane = lax.broadcasted_iota(jnp.int32, shape, 2)
    column = lax.broadcasted_iota(jnp.int32, shape, 0)
    depth = lane & (edge - 1)
    low_depth = depth == 0
    high_depth = depth == edge - 1
    low_lane = lane < edge
    high_lane = lane >= LANES - edge
    low_row = low_lane & (column == 0)
    high_row = high_lane & (column == columns - 1)
    edge_masks = (None, None, low_row, high_row, low_depth, high_depth)
    parity = (
        lax.broadcasted_iota(jnp.int32, shape, 1)
        + column * (LANES // edge)
        + (lane >> (edge.bit_length() - 1))
        + depth
    ) & 1
    plane_shape = (columns, 1, LANES)
    plane_lane = lax.broadcasted_iota(jnp.int32, plane_shape, 2)
    plane_parity = (
        lax.broadcasted_iota(jnp.int32, plane_shape, 0) * (LANES // edge)
        + (plane_lane >> (edge.bit_length() - 1))
        + (plane_lane & (edge - 1))
    ) & 1
    pairs = columns // 2
    even_line = ((lane[:pairs] >> (edge.bit_length() - 1)) & 1) == 0
    odd_cell = parity[:pairs] == 1

    def spread(rows):
        return jnp.stack([rows[:, c * LANES : (c + 1) * LANES] for c in range(columns)])

    def flatten(block):
        return jnp.concatenate([block[c] for c in range(columns)], axis=1)

    def thin(block, colour):
        low, high = block[:pairs], block[pairs:]
        low_next = pltpu.roll(low, LANES - edge, 2)
        high_next = pltpu.roll(high, edge, 2)
        if colour:
            low = jnp.where(odd_cell, low, low_next)
            high = jnp.where(odd_cell, high, high_next)
        else:
            low = jnp.where(odd_cell, low_next, low)
            high = jnp.where(odd_cell, high_next, high)
        return jnp.where(even_line, low, high)

    def thicken(block):
        low = jnp.where(even_line, block, pltpu.roll(block, edge, 2))
        high = jnp.where(even_line, pltpu.roll(block, LANES - edge, 2), block)
        return jnp.concatenate([low, high], axis=0)

    for table in tables:
        table.wait()
    start = jnp.int32(0)
    for other in range(curve):
        start = start + jnp.where(other < place, count_ref[0, other], 0)
    end = start
    for other in range(curve):
        end = end + jnp.where(other == place, count_ref[0, other], 0)
    first = place * boxes
    right_slot = jnp.clip(first + boxes - start, 0, slots - 1)
    own_slots = [jnp.clip(first + b - start, 0, slots - 1) for b in range(boxes)]
    load(2).wait()
    for side, slot in ((0, 0), (1, right_slot)):
        coef_out[side] = held_coef[slot]
    pl.semaphore_wait(
        barrier, groups - 1 + has_left.astype(jnp.int32) + has_right.astype(jnp.int32)
    )

    def move(side, part):
        if part == 0:
            source, target = coef_out.at[side], coef_in.at[side]
        elif part == 1:
            source, target = half_out.at[side], half_in.at[side]
        else:
            source, target = rows_out.at[part - 2, side], rows_in.at[part - 2, side]
        return pltpu.make_async_remote_copy(
            src_ref=source,
            dst_ref=target,
            send_sem=move_send.at[side, part],
            recv_sem=move_recv.at[side, part],
            device_id=(place + 2 * side - 1, group),
            device_id_type=MESH,
        )

    def move_start(part):
        @pl.when(has_left)
        def _():
            move(0, part).start()

        @pl.when(has_right)
        def _():
            move(1, part).start()

    outer = [0, tiles - 1]
    inner = list(range(1, tiles - 1))
    move_start(0)
    load(0).wait()
    for side, slot in ((0, 0), (1, right_slot)):
        for t in range(tiles):
            rows = slice(t * TILE, (t + 1) * TILE)
            half_out[side, :, rows, :] = thin(spread(held_sol[slot, rows, :]), 1)
    move_start(1)
    load(1).wait()
    for side, slot in ((0, 0), (1, right_slot)):
        for part, which in ((0, outer), (1, inner)):
            for i, t in enumerate(which):
                rows_out[part, side, i] = held_rhs[slot, t * TILE : (t + 1) * TILE, :]
    move_start(2)

    def move_wait(part):
        @pl.when(has_right)
        def _():
            move(0, part).wait_recv()

        @pl.when(has_left)
        def _():
            move(1, part).wait_recv()

    def moved(field, b, t, arrived):
        rows = slice(t * TILE, (t + 1) * TILE)
        block = spread(held[field][own_slots[b], rows, :])
        if b == 0:
            block = jnp.where(first + b < start, arrived(1, rows), block)
        if b == boxes - 1:
            block = jnp.where(first + b >= end, arrived(0, rows), block)
        return block

    def face_to(k, side):
        return pltpu.make_async_remote_copy(
            src_ref=face_out.at[k, side],
            dst_ref=face_in.at[k, side],
            send_sem=face_send.at[k, side],
            recv_sem=face_recv.at[k, side],
            device_id=(place + 2 * side - 1, group),
            device_id_type=MESH,
        )

    def faces_start(k, plane_of):
        for b in range(boxes):
            for side in range(2):
                face_out[k, side, b] = plane_of(b, side)

        @pl.when(has_left)
        def _():
            face_to(k, 0).start()

        @pl.when(has_right)
        def _():
            face_to(k, 1).start()

    def faces_wait(k):
        @pl.when(has_left)
        def _():
            face_to(k, 1).wait_recv()

        @pl.when(has_right)
        def _():
            face_to(k, 0).wait_recv()

    def own_planes(ref):
        return lambda b, side: ref[
            b, :, PAD + side * (edge - 1) : PAD + side * (edge - 1) + 1, :
        ]

    links = [[link_ref[0, b, f] for f in range(FACES)] for b in range(boxes)]
    linked = [[jnp.where(t >= 0, 1.0, 0.0) for t in row] for row in links]
    beside = [[jnp.clip(t - first, 0, boxes - 1) for t in row] for row in links]

    def arrived_plane(k, b, f, plane):
        base = first + (2 * f - 1) * boxes
        for other in range(boxes):
            plane = jnp.where(
                (links[b][f] >= 0) & (links[b][f] == base + other),
                face_in[k, 1 - f, other],
                plane,
            )
        return plane

    no_plane = jnp.zeros((columns, 1, LANES), jnp.float32)
    ghost_at = (PAD - 1, PAD + edge)

    def ghost_rows(k, ref, keep_own):
        for b in range(boxes):
            for f in range(2):
                plane = own_planes(ref)(b, f) if keep_own else no_plane
                ref[b, :, ghost_at[f] : ghost_at[f] + 1, :] = arrived_plane(k, b, f, plane)

    def advance_ghosts(colour):
        for b in range(boxes):
            for f in range(2):
                row = slice(ghost_at[f], ghost_at[f] + 1)
                plane = sol[b, :, row, :]
                sol[b, :, row, :] = jnp.where(
                    ((plane_parity + 1 - f) & 1) == colour,
                    plane + arrived_plane(2, b, f, no_plane) * own_planes(sol)(b, f),
                    plane,
                )

    def around(ref, b, t):
        rows = slice(PAD + t * TILE, PAD + (t + 1) * TILE)
        here = ref[b, :, rows, :]
        low_y = pltpu.roll(here, edge, 2)
        high_y = pltpu.roll(here, LANES - edge, 2)
        ghost_low = pltpu.roll(ref[beside[b][2], columns - 1, rows, :], edge, 1)
        ghost_high = pltpu.roll(ref[beside[b][3], 0, rows, :], LANES - edge, 1)
        before = jnp.concatenate([ghost_low[None], low_y[:-1]], axis=0)
        after = jnp.concatenate([high_y[1:], ghost_high[None]], axis=0)
        return here, (
            ref[b, :, PAD + t * TILE - 1 : PAD + (t + 1) * TILE - 1, :],
            ref[b, :, PAD + t * TILE + 1 : PAD + (t + 1) * TILE + 1, :],
            jnp.where(low_lane, before, low_y),
            jnp.where(high_lane, after, high_y),
            jnp.where(
                low_depth,
                pltpu.roll(ref[beside[b][4], :, rows, :], LANES - edge + 1, 2),
                pltpu.roll(here, 1, 2),
            ),
            jnp.where(
                high_depth,
                pltpu.roll(ref[beside[b][5], :, rows, :], edge - 1, 2),
                pltpu.roll(here, LANES - 1, 2),
            ),
        )

    target = lax.broadcasted_iota(jnp.int32, merge_map.shape, 0)
    target = ((target >> edge.bit_length()) * half) + (
        (target & (edge - 1)) >> 1
    )
    merge_map[...] = jnp.where(
        target == lax.broadcasted_iota(jnp.int32, merge_map.shape, 1), 1.0, 0.0
    ).astype(jnp.bfloat16)
    for b in range(boxes):
        label = (
            parent_ref[0, b, 0] * coarse_slots + parent_ref[0, b, 1] * 8 + parent_ref[0, b, 2]
        ).astype(jnp.float32)
        pack[b, half : half + TILE, :] = jnp.full((TILE, half * half), label, jnp.float32)

    move_wait(0)
    for b in range(boxes):
        for t in range(tiles):
            coef[b, :, PAD + t * TILE : PAD + (t + 1) * TILE, :] = moved(
                2, b, t, lambda side, rows: spread(coef_in[side, rows, :])
            )
    faces_start(0, own_planes(coef))
    move_start(3)
    move_wait(1)
    for b in range(boxes):
        for t in range(tiles):
            sol[b, :, PAD + t * TILE : PAD + (t + 1) * TILE, :] = moved(
                0, b, t, lambda side, rows: thicken(half_in[side, :, rows, :])
            )
    faces_start(1, own_planes(sol))
    faces_wait(0)
    ghost_rows(0, coef, True)
    for b in range(boxes):
        for t in range(tiles):
            here, near = around(coef, b, t)
            total = jnp.full(shape, MASS_TERM, jnp.float32)
            kept = []
            for f in range(FACES):
                beyond = near[f]
                if f >= 2:
                    inside = linked[b][f]
                    beyond = jnp.where(
                        edge_masks[f], beyond * inside + here * (1.0 - inside), beyond
                    )
                weight = 0.5 * (here + beyond)
                total = total + weight
                if f >= 2:
                    weight = jnp.where(edge_masks[f], weight * linked[b][f], weight)
                kept.append(weight)
            over = 1.0 / total
            diagonal[b, t] = total
            inverse[b, t] = over
            for f in range(FACES):
                weights[b, t, f] = kept[f] * over

    faces_start(
        2,
        lambda b, side: weights[
            b, side * (tiles - 1), side, :, side * (TILE - 1) : side * (TILE - 1) + 1, :
        ],
    )

    def scale_rhs(part, which):
        move_wait(part)
        for b in range(boxes):
            for i, t in enumerate(which):
                scaled_rhs[b, t] = inverse[b, t] * moved(
                    1, b, t, lambda side, rows, i=i: spread(rows_in[part - 2, side, i])
                )

    def relaxed(b, t):
        here, near = around(sol, b, t)
        total = scaled_rhs[b, t]
        for f in range(FACES):
            total = total + weights[b, t, f] * near[f]
        return here, total

    def sweep(colour, which):
        for b in range(boxes):
            for t in which:
                here, total = relaxed(b, t)
                sol[b, :, PAD + t * TILE : PAD + (t + 1) * TILE, :] = jnp.where(
                    parity == colour, total, here
                )

    def next_planes(colour):
        def plane_of(b, side):
            t = side * (tiles - 1)
            here, near = around(sol, b, t)
            total = scaled_rhs[b, t]
            for f in range(FACES):
                if f != side:
                    total = total + weights[b, t, f] * near[f]
            block = jnp.where(parity == colour, total, here)
            return block[:, side * (TILE - 1) : side * (TILE - 1) + 1, :]

        return plane_of

    faces_wait(1)
    ghost_rows(1, sol, False)
    scale_rhs(2, outer)
    sweep(0, outer)
    faces_start(3, next_planes(1))
    scale_rhs(3, inner)
    sweep(0, inner)
    sweep(1, inner)
    faces_wait(2)
    faces_wait(3)
    ghost_rows(3, sol, False)
    sweep(1, outer)
    advance_ghosts(1)
    sweep(0, outer)
    faces_start(4, next_planes(1))
    sweep(0, inner)
    sweep(1, inner)
    faces_wait(4)
    ghost_rows(4, sol, False)
    sweep(1, outer)
    advance_ghosts(1)

    def leave(which):
        for b in range(boxes):
            for t in which:
                here, total = relaxed(b, t)
                res_rows[b, t * TILE : (t + 1) * TILE, :] = flatten(
                    diagonal[b, t] * (total - here)
                )

    leave(range(tiles))
    residual_store = pltpu.make_async_copy(res_rows, residual_out.at[0], store_sem.at[1])
    residual_store.start()

    for b in range(boxes):
        rows = res_rows[b]
        high = rows.astype(jnp.bfloat16)
        low = (rows - high.astype(jnp.float32)).astype(jnp.bfloat16)
        both = jnp.dot(
            jnp.concatenate([high, low], axis=0),
            merge_map[...],
            preferred_element_type=jnp.float32,
        )
        both = both[:edge] + both[edge:]
        for c in range(merged.shape[1]):
            merged[b, c] = both[:, c * LANES : (c + 1) * LANES]
    for b in range(boxes):
        for c in range(merged.shape[1]):
            pack[b, 0:half, c * LANES : (c + 1) * LANES] = 0.125 * (
                merged[b, c, pl.ds(0, half, stride=2), :]
                + merged[b, c, pl.ds(1, half, stride=2), :]
            )

    def pack_to(step):
        return pltpu.make_async_remote_copy(
            src_ref=pack,
            dst_ref=packs_out.at[step],
            send_sem=pack_send.at[step - 1],
            recv_sem=pack_recv.at[step - 1],
            device_id=(place, lax.rem(group + step, groups)),
            device_id_type=MESH,
        )

    for step in range(1, groups):
        pack_to(step).start()
    for b in range(boxes):
        for t in range(tiles):
            plane_out[b, t * TILE : (t + 1) * TILE, :] = flatten(
                sol[b, :, PAD + t * TILE : PAD + (t + 1) * TILE, :]
            )
    smooth_store = pltpu.make_async_copy(plane_out, smooth_out.at[0], store_sem.at[0])
    smooth_store.start()
    own_store = pltpu.make_async_copy(pack, packs_out.at[0], store_sem.at[2])
    own_store.start()
    for step in range(1, groups):
        pack_to(step).wait_recv()

    for step in range(1, groups):
        pack_to(step).wait_send()

    @pl.when(has_left)
    def _():
        for part in range(4):
            move(0, part).wait_send()
        for k in range(5):
            face_to(k, 0).wait_send()

    @pl.when(has_right)
    def _():
        for part in range(4):
            move(1, part).wait_send()
        for k in range(5):
            face_to(k, 1).wait_send()

    smooth_store.wait()
    residual_store.wait()
    own_store.wait()


def hand_out_kernel(
    smooth_in,
    residual_in,
    packs_in,
    coarse_in,
    smooth_out,
    residual_out,
    coarse_out,
    smooth_buf,
    residual_buf,
    packs,
    coarse,
    load_sem,
    store_sem,
):
    group = lax.axis_index("grp")
    groups, boxes = packs.shape[:2]
    slots, half = coarse.shape[:2]
    loads = [
        pltpu.make_async_copy(source, target, load_sem.at[i])
        for i, (source, target) in enumerate(
            (
                (packs_in, packs),
                (coarse_in, coarse),
                (smooth_in, smooth_buf),
                (residual_in, residual_buf),
            )
        )
    ]
    stores = [
        pltpu.make_async_copy(source, target, store_sem.at[i])
        for i, (source, target) in enumerate(
            ((smooth_buf, smooth_out), (residual_buf, residual_out), (coarse, coarse_out))
        )
    ]
    for load in loads:
        load.start()
    loads[0].wait()
    loads[1].wait()
    for source in range(groups):
        for b in range(boxes):
            label = packs[source, b, half : half + TILE, :]
            label = jnp.concatenate([label] * (half // TILE), axis=0)
            values = packs[source, b, 0:half, :]
            for s in range(slots):
                mine = (group * slots + s).astype(jnp.float32)
                coarse[s] = jnp.where(label == mine, values, coarse[s])
    stores[2].start()
    for i in range(2):
        loads[2 + i].wait()
        stores[i].start()
    for store in stores:
        store.wait()


def per_device(old_fields, old_count, neighbours, parents, coarse_source):
    _, _, slots, edge, cells = old_fields.shape
    boxes = neighbours.shape[1]
    groups = lax.axis_size("grp")
    _, coarse_boxes, octants, half, quarter = coarse_source.shape
    tiles = edge // TILE
    columns = cells // LANES
    padded = edge + 2 * PAD
    f32 = jnp.float32
    coarse_slots = coarse_boxes * octants
    scratch = [
        pltpu.SMEM(old_count.shape, jnp.int32),
        pltpu.SMEM(neighbours.shape, jnp.int32),
        pltpu.SMEM(parents.shape, jnp.int32),
        pltpu.VMEM((slots, edge, cells), f32),
        pltpu.VMEM((slots, edge, cells), f32),
        pltpu.VMEM((slots, edge, cells), f32),
        pltpu.VMEM((2, edge, cells), f32),
        pltpu.VMEM((2, edge, cells), f32),
        pltpu.VMEM((2, columns // 2, edge, LANES), f32),
        pltpu.VMEM((2, columns // 2, edge, LANES), f32),
        pltpu.VMEM((2, 2, tiles // 2, TILE, cells), f32),
        pltpu.VMEM((2, 2, tiles // 2, TILE, cells), f32),
        pltpu.VMEM((boxes, columns, padded, LANES), f32),
        pltpu.VMEM((boxes, columns, padded, LANES), f32),
        pltpu.VMEM((boxes, tiles, FACES, columns, TILE, LANES), f32),
        pltpu.VMEM((boxes, tiles, columns, TILE, LANES), f32),
        pltpu.VMEM((boxes, tiles, columns, TILE, LANES), f32),
        pltpu.VMEM((boxes, tiles, columns, TILE, LANES), f32),
        pltpu.VMEM((boxes, edge, cells), f32),
        pltpu.VMEM((boxes, edge, cells), f32),
        pltpu.VMEM((cells, quarter), jnp.bfloat16),
        pltpu.VMEM((boxes, quarter // LANES, edge, LANES), f32),
        pltpu.VMEM((boxes, half + TILE, quarter), f32),
        pltpu.VMEM((5, 2, boxes, columns, 1, LANES), f32),
        pltpu.VMEM((5, 2, boxes, columns, 1, LANES), f32),
        pltpu.SemaphoreType.DMA((6,)),
        pltpu.SemaphoreType.DMA((2, 4)),
        pltpu.SemaphoreType.DMA((2, 4)),
        pltpu.SemaphoreType.DMA((5, 2)),
        pltpu.SemaphoreType.DMA((5, 2)),
        pltpu.SemaphoreType.DMA((groups - 1,)),
        pltpu.SemaphoreType.DMA((groups - 1,)),
        pltpu.SemaphoreType.DMA((3,)),
    ]
    anywhere = pl.BlockSpec(memory_space=pl.ANY)
    in_hbm = pl.BlockSpec(memory_space=pltpu.HBM)
    smoothed, residual, packs = pl.pallas_call(
        functools.partial(level_kernel, coarse_slots),
        out_shape=(
            jax.ShapeDtypeStruct((1, boxes, edge, cells), f32),
            jax.ShapeDtypeStruct((1, boxes, edge, cells), f32),
            jax.ShapeDtypeStruct((groups, boxes, half + TILE, quarter), f32),
        ),
        in_specs=[in_hbm] * 4,
        out_specs=(anywhere, anywhere, anywhere),
        scratch_shapes=scratch,
        compiler_params=pltpu.CompilerParams(
            collective_id=0, has_side_effects=True, vmem_limit_bytes=VMEM_BYTES
        ),
    )(
        old_fields,
        old_count,
        neighbours,
        parents,
    )
    coarse = coarse_source.reshape(coarse_slots, half, quarter)
    parts = (smoothed, residual, packs, coarse)
    results = (smoothed, residual, coarse)
    smoothed, residual, coarse_rhs = pl.pallas_call(
        hand_out_kernel,
        out_shape=tuple(jax.ShapeDtypeStruct(part.shape, f32) for part in results),
        in_specs=[in_hbm] * 4,
        out_specs=(in_hbm,) * 3,
        scratch_shapes=[pltpu.VMEM(part.shape, f32) for part in parts]
        + [pltpu.SemaphoreType.DMA((4,)), pltpu.SemaphoreType.DMA((3,))],
        compiler_params=pltpu.CompilerParams(vmem_limit_bytes=VMEM_BYTES),
    )(*parts)
    return smoothed, residual, coarse_rhs.reshape(coarse_source.shape)


def solution(mesh):
    in_specs = (
        P(None, "grp", "box", None, None),
        P("grp", None),
        P("grp", "box", None),
        P("grp", "box", None),
        P("grp", "box", None, None, None),
    )
    out_specs = (
        P("grp", "box", None, None),
        P("grp", "box", None, None),
        P("grp", "box", None, None, None),
    )
    return jax.shard_map(
        per_device, mesh=mesh, in_specs=in_specs, out_specs=out_specs, check_vma=False
    )
```
